512 devices in a mesh: segment: 64 (over x, z_lo, core), slab: 8 (over y, z_hi).
Axes of the slice: x: 4, y: 4, z: 16 (z_hi: 2, z_lo: 8; z = z_hi * 8 + z_lo), core: 2. Of those that a mesh axis runs over, the one named last changes fastest.
Arguments:
- fwd_in: bfloat16 [64, 2, 32, 16, 4, 128], P('segment', None, None, 'slab'), may hold values from -6 to 6
- back_out: bfloat16 [64, 2, 32, 16, 4, 128], P('segment', None, None, 'slab'), may hold values from -6 to 6
- back_grad: bfloat16 [64, 2, 32, 16, 4, 128], P('segment', None, None, 'slab'), may hold values from -6 to 6
- batch_next: bfloat16 [2, 32, 16, 4, 128], P(None, None, 'slab'), may hold values from -6 to 6
- loss_grad: bfloat16 [2, 2, 32, 16, 4, 128], P(None, None, None, 'slab'), may hold values from -6 to 6
- weights: bfloat16 [64, 2, 32, 864], P('segment'), may hold values from -0.21875 to 0.21875
Outputs:
- fwd_out: bfloat16 [64, 2, 32, 16, 4, 128], P('segment', None, None, 'slab')
- back_acts: bfloat16 [64, 2, 32, 16, 4, 128], P('segment', None, None, 'slab')
- back_grads: bfloat16 [64, 2, 32, 16, 4, 128], P('segment', None, None, 'slab')
- weight_grads: float32 [64, 2, 32, 864], P('segment', None, None, 'slab')
The draws below stay inside these ranges and needn't reach their ends.
All inputs are finite; a program needn't handle non-finite values.
Results may differ from the reference program's by a relative error of at most 0.012.
Values may be sent and summed in bfloat16 or wider, within the bound.
No kernel may reach another device: no remote copies, remote signals or barrier semaphores. Data moves between devices by JAX's collectives and lax.ppermute only.
A program may use at most 64 MiB of HBM per device.

```python
import jax
import jax.numpy as jnp
from jax import lax

C = 32
PLANE_H = 4
PLANE_W = 128
SEGMENTS = 64
DEPTH = 16
CELLS = 8192


def steps_of(key, dims, cuts, least, high):
    gain = 1.0
    for dim, parts in cuts:
        steps = jax.random.uniform(jax.random.fold_in(jax.random.fold_in(key, 6), dim), (parts,), jnp.float32, least / len(cuts), high / len(cuts))
        gain = gain * jnp.repeat(jnp.exp(steps), dims[dim] // parts).reshape((-1,) + (1,) * (len(dims) - 1 - dim))
    return gain


def noise(rng, dims, scale, bound, split=(), kind=jnp.bfloat16):
    array = scale * jax.random.normal(rng, dims, jnp.float32)
    if split:
        array = array * steps_of(rng, dims, split, -0.22, 0.18)
    return jnp.clip(array, -bound, bound).astype(kind)


def setup_inputs(seed: int = 0) -> dict:
    streams_of = jax.random.split(jax.random.key(seed), 7)
    return {
        "fwd_in": noise(streams_of[0], (SEGMENTS, 2, C, DEPTH, PLANE_H, PLANE_W), 1.0, 6.0, ((0, 64), (3, 8))),
        "back_out": noise(streams_of[1], (SEGMENTS, 2, C, DEPTH, PLANE_H, PLANE_W), 1.0, 6.0, ((0, 64), (3, 8))),
        "back_grad": noise(streams_of[2], (SEGMENTS, 2, C, DEPTH, PLANE_H, PLANE_W), 1.0, 6.0, ((0, 64), (3, 8))),
        "batch_next": noise(streams_of[3], (2, C, DEPTH, PLANE_H, PLANE_W), 1.0, 6.0, ((2, 8),)),
        "loss_grad": noise(streams_of[4], (2, 2, C, DEPTH, PLANE_H, PLANE_W), 1.0, 6.0, ((3, 8),)),
        "weights": noise(streams_of[5], (SEGMENTS, 2, C, 27 * C), (27 * C) ** -0.5, 0.21875, ((0, 64),)),
    }


def silu_round(value):
    return jax.nn.silu(value.astype(jnp.float32)).astype(jnp.bfloat16)

def silu_slope(value):
    wide = value.astype(jnp.float32)
    sig = jax.nn.sigmoid(wide)
    return sig * (1.0 + wide * (1.0 - sig))

def kernel_of(flat):
    chan = flat.shape[0]
    return flat.reshape(chan, chan, 3, 3, 3)

def conv_full(field, flat):
    out = lax.conv_general_dilated(field[None], kernel_of(flat), (1, 1, 1), ((1, 1), (1, 1), (1, 1)), dimension_numbers=('NCDHW', 'OIDHW', 'NCDHW'), preferred_element_type=jnp.float32)
    return out[0]

def conv_back(grad, flat):
    turned = jnp.flip(kernel_of(flat), (2, 3, 4)).transpose(1, 0, 2, 3, 4)
    out = lax.conv_general_dilated(grad[None], turned, (1, 1, 1), ((1, 1), (1, 1), (1, 1)), dimension_numbers=('NCDHW', 'OIDHW', 'NCDHW'), preferred_element_type=jnp.float32)
    return out[0]

def weight_grad(grad, field):
    padded = jnp.pad(field, ((0, 0), (1, 1), (1, 1), (1, 1)))
    out = lax.conv_general_dilated(padded[:, None], grad[:, None], (1, 1, 1), 'VALID', dimension_numbers=('NCDHW', 'OIDHW', 'NCDHW'), preferred_element_type=jnp.float32)
    out = out.transpose(1, 0, 2, 3, 4)
    return out.reshape(out.shape[0], -1)

def section(inputs):
    fin, back_pair, back_cot, wts = inputs
    x1 = fin[0]
    x2 = fin[1]
    y1 = (x1.astype(jnp.float32) + conv_full(silu_round(x2), wts[0])).astype(jnp.bfloat16)
    y2 = (x2.astype(jnp.float32) + conv_full(silu_round(y1), wts[1])).astype(jnp.bfloat16)
    out1 = back_pair[0]
    out2 = back_pair[1]
    grad1 = back_cot[0]
    grad2 = back_cot[1]
    hidden = silu_round(out1)
    rec2 = (out2.astype(jnp.float32) - conv_full(hidden, wts[1])).astype(jnp.bfloat16)
    act2 = silu_round(rec2)
    rec1 = (out1.astype(jnp.float32) - conv_full(act2, wts[0])).astype(jnp.bfloat16)
    grad_one = (grad1.astype(jnp.float32) + silu_slope(out1) * conv_back(grad2, wts[1])).astype(jnp.bfloat16)
    grad_two = (grad2.astype(jnp.float32) + silu_slope(rec2) * conv_back(grad_one, wts[0])).astype(jnp.bfloat16)
    scale = float(CELLS) ** (-0.5)
    dweights = jnp.stack([weight_grad(grad_one, act2), weight_grad(grad2, hidden)]) * scale
    return (jnp.stack([y1, y2]), jnp.stack([rec1, rec2]), jnp.stack([grad_one, grad_two]), dweights)

def reference(fwd_in, back_out, back_grad, batch_next, loss_grad, weights):
    fout1, rec1, din1, dw1 = lax.map(section, (fwd_in, back_out, back_grad, weights))
    fin2 = jnp.concatenate([batch_next[None], fout1[:-1]], axis=0)
    acts2 = jnp.concatenate([rec1[1:], fout1[-1:]], axis=0)
    grads2 = jnp.concatenate([din1[1:], loss_grad[0][None]], axis=0)
    fout2, rec2, din2, dw2 = lax.map(section, (fin2, acts2, grads2, weights))
    back_acts = jnp.concatenate([rec2[1:], fout2[-1:]], axis=0)
    back_grads = jnp.concatenate([din2[1:], loss_grad[1][None]], axis=0)
    return (fout2, back_acts, back_grads, dw1 + dw2)
```

```python
import functools

import jax
import jax.numpy as jnp
from jax import lax
from jax.experimental import pallas as pl
from jax.experimental.pallas import tpu as pltpu
from jax.sharding import PartitionSpec as P

F32 = jnp.float32
BF16 = jnp.bfloat16
C = 32
H = 4
R = C * H
W = 128
SNAKE = 16


def wide(v):
    return v.astype(F32)


def silu(v):
    v = wide(v)
    return (v / (1.0 + jnp.exp(-v))).astype(BF16)


def slope(v):
    v = wide(v)
    sig = 1.0 / (1.0 + jnp.exp(-v))
    return sig * (1.0 + v * (1.0 - sig))


def conv_planes(w_ref, field, start, count, use):
    lane = lax.broadcasted_iota(jnp.int32, (R, W), 1)
    d = start
    while d < start + count:
        n = min(2, start + count - d)
        x = jnp.concatenate(
            [jnp.concatenate([field[d + k + a] for a in range(3)], axis=0) for k in range(n)], axis=1
        )
        y = jnp.dot(w_ref[...], x, preferred_element_type=F32)
        for k in range(n):
            cols = slice(k * W, (k + 1) * W)
            left = jnp.where(lane >= 1, pltpu.roll(y[:R, cols], 1, 1), 0.0)
            right = jnp.where(lane < W - 1, pltpu.roll(y[2 * R :, cols], W - 1, 1), 0.0)
            use(d + k, y[R : 2 * R, cols] + left + right)
        d += n


def stages(n, keep_lo, keep_hi, w_ref, fb, fa, bb, ba, db, da, fo_a, fo_b, bo_a, bo_b, go_a, go_b, act_b, act_a):
    inner = n - 2

    def mask(d, v):
        if d == 0:
            v = v * keep_lo
        if d == inner - 1:
            v = v * keep_hi
        return v

    def fwd():
        for p in range(n):
            act_b[p] = silu(fb[p])

        def one(d, v):
            out = mask(d, wide(fa[d]) + v).astype(BF16)
            fo_a[d] = out
            act_a[d] = silu(out)

        conv_planes(w_ref.at[0], act_b, 0, inner, one)

        def two(d, v):
            fo_b[d] = (wide(fb[d + 2]) + v).astype(BF16)

        conv_planes(w_ref.at[1], act_a, 0, inner - 2, two)

    def back():
        for p in range(n):
            act_b[p] = silu(bb[p])

        def rec_a(d, v):
            out = mask(d, wide(ba[d]) - v).astype(BF16)
            bo_a[d] = out
            act_a[d] = silu(out)

        conv_planes(w_ref.at[1], act_b, 0, inner, rec_a)

        def grad_a(d, v):
            go_a[d] = mask(d, wide(da[d]) + slope(bb[d + 1]) * v).astype(BF16)

        conv_planes(w_ref.at[3], db, 0, inner, grad_a)

        def rec_b(d, v):
            bo_b[d] = (wide(bb[d + 2]) - v).astype(BF16)

        conv_planes(w_ref.at[0], act_a, 0, inner - 2, rec_b)

        def grad_b(d, v):
            go_b[d] = (wide(db[d + 2]) + slope(bo_a[d + 1]) * v).astype(BF16)

        conv_planes(w_ref.at[2], go_a, 0, inner - 2, grad_b)

    fwd()
    back()


def put(win, at, piece):
    for k in range(piece.shape[0]):
        win[at + k] = piece[k]


def tick1_kernel(flags, w_ref, nat, swp, yn, yf, fm, fd, bm, bd, ld, y1w, h4, u4, e1p, *scratch):
    fb, fa, bb, ba, db, da, fo_b, bo_a, bo_b, go_a, go_b, act_b, act_a = scratch
    zh, keep_lo, keep_hi, fz, bz = (flags[k] for k in range(5))
    for k, win in enumerate((fb, bb, db)):
        put(win, 2 + 2 * zh, nat.at[k])
        put(win, 4 - 2 * zh, swp.at[k])
        put(win, 6 - 6 * zh, yn.at[pl.ds(2 * k, 2)])
        put(win, 6 * zh, yf.at[pl.ds(2 * k, 2)])
    for k, win in enumerate((fa, ba, da)):
        put(win, 1 + 2 * zh, nat.at[3 + k])
        put(win, 3 - 2 * zh, swp.at[3 + k])
        put(win, 5 - 5 * zh, yn.at[pl.ds(6 + k, 1)])
        put(win, 5 * zh, yf.at[pl.ds(6 + k, 1)])
    stages(
        8, keep_lo.astype(F32), keep_hi.astype(F32), w_ref, fb, fa, bb, ba, db, da,
        y1w, fo_b, bo_a, bo_b, go_a, go_b, act_b, act_a,
    )
    for k in range(4):
        fm[k] = fo_b[k]
        fm[4 + k] = y1w[2 * fz + k]
        bm[k] = bo_b[k]
        bm[4 + k] = go_b[k]
        bm[8 + k] = bo_a[2 * bz + k]
        bm[12 + k] = go_a[2 * bz + k]
        h4[k] = act_b[1 + 2 * zh + k]
        u4[k] = act_a[2 * zh + k]
    for k in range(2):
        fd[k] = fo_b[2 - 2 * fz + k]
        bd[k] = bo_b[2 - 2 * bz + k]
        bd[2 + k] = go_b[2 - 2 * bz + k]
        e1p[k] = go_a[1 + 2 * zh + k]
    ld[zh] = y1w[3 - zh]
    ld[1 - zh] = fo_b[3 - 3 * zh]


def tick2_kernel(
    flags, w_ref, fm, fd, bm, bd, sp1, sp2, first_own, last_own, y1w, own, ld, out_f, out_b, h4, u4, e1p, d2p, *scratch
):
    fb, fa, bb, ba, db, da, fo_a, fo_b, bo_a, bo_b, go_a, go_b, act_b, act_a = scratch
    zh, keep_lo, keep_hi, first, last = (flags[k] for k in range(5))
    main, halo = (2 - 2 * zh, 4 * zh)

    def special(b_win, a_win, own):
        put(b_win, 2, own.at[1])
        put(b_win, 4 - 4 * zh, sp1.at[1])
        put(b_win, 4 * zh, sp2.at[1])
        put(a_win, 1, own.at[0])
        a_win[3 - 3 * zh] = sp1[0, zh]
        a_win[3 * zh] = sp2[0, 1 - zh]

    @pl.when(first == 1)
    def _():
        special(fb, fa, first_own)

    @pl.when(first == 0)
    def _():
        put(fb, main, fm.at[pl.ds(0, 4)])
        put(fb, halo, fd)
        put(fa, 0, fm.at[pl.ds(4, 4)])

    @pl.when(last == 1)
    def _():
        special(db, da, last_own)
        for k in range(5):
            bb[1 - zh + k] = y1w[zh + k]
        bb[5 * zh] = ld[zh]
        for k in range(3):
            ba[1 - zh + k] = own[zh + k]
        ba[3 * zh] = ld[1 - zh]

    @pl.when(last == 0)
    def _():
        put(bb, main, bm.at[pl.ds(0, 4)])
        put(bb, halo, bd.at[pl.ds(0, 2)])
        put(db, main, bm.at[pl.ds(4, 4)])
        put(db, halo, bd.at[pl.ds(2, 2)])
        put(ba, 0, bm.at[pl.ds(8, 4)])
        put(da, 0, bm.at[pl.ds(12, 4)])

    stages(
        6, keep_lo.astype(F32), keep_hi.astype(F32), w_ref, fb, fa, bb, ba, db, da,
        fo_a, fo_b, bo_a, bo_b, go_a, go_b, act_b, act_a,
    )
    for k in range(2):
        out_f[k] = fo_a[1 + k]
        out_f[2 + k] = fo_b[k]
        out_b[k] = bo_b[k]
        out_b[2 + k] = bo_a[1 + k]
        out_b[4 + k] = go_a[1 + k]
        out_b[6 + k] = go_b[k]
        e1p[k] = go_a[1 + k]
        d2p[k] = db[2 + k]
    for k in range(4):
        h4[k] = act_b[1 + k]
        u4[k] = act_a[k]


def wgrad_pair(g_ref, u_ref):
    lane = lax.broadcasted_iota(jnp.int32, (C, W), 1)
    zero = jnp.zeros((C, W), BF16)
    left, right = ([], [])
    for d in range(2):
        for h in range(H):
            g = wide(g_ref[d, h * C : (h + 1) * C])
            down = jnp.where(lane < W - 1, pltpu.roll(g, W - 1, 1), 0.0)
            up = jnp.where(lane >= 1, pltpu.roll(g, 1, 1), 0.0)
            left.append(jnp.concatenate([down, g, up], axis=0).astype(BF16))
            rows = []
            for a in range(3):
                for b in range(3):
                    at = h + b - 1
                    rows.append(u_ref[d + a, at * C : (at + 1) * C] if 0 <= at < H else zero)
            right.append(jnp.concatenate(rows, axis=0))
    return lax.dot_general(
        jnp.concatenate(left, axis=1),
        jnp.concatenate(right, axis=1),
        (((1,), (1,)), ((), ())),
        preferred_element_type=F32,
    )


def wgrad_kernel(e1, u4, d2, h4, out):
    out[0] = wgrad_pair(e1, u4)
    out[1] = wgrad_pair(d2, h4)


def wgrad_add_kernel(scale, e1, u4, d2, h4, prev, out):
    out[0] = (prev[0] + wgrad_pair(e1, u4)) * scale
    out[1] = (prev[1] + wgrad_pair(d2, h4)) * scale


VMEM = pl.BlockSpec(memory_space=pltpu.VMEM)
SMEM = pl.BlockSpec(memory_space=pltpu.SMEM)


def call(kernel, outs, scratch, args, flops, flagged=True):
    n = len(args)
    return pl.pallas_call(
        kernel,
        out_shape=tuple(jax.ShapeDtypeStruct(s, t) for s, t in outs),
        in_specs=([SMEM] + [VMEM] * (n - 1)) if flagged else [VMEM] * n,
        out_specs=tuple(VMEM for _ in outs),
        scratch_shapes=scratch,
        compiler_params=pltpu.CompilerParams(vmem_limit_bytes=40 * 2**20),
        cost_estimate=pl.CostEstimate(flops=flops, bytes_accessed=4_000_000, transcendentals=400_000),
    )(*args)


def planes(*lead):
    return pltpu.VMEM((*lead, R, W), BF16)


def shaped(*lead):
    return ((*lead, R, W), BF16)


def inside(value):
    s, _, d = value.shape[:3]
    return value.transpose(0, 2, 3, 1, 4).reshape(s, d, R, W)


def outside(value):
    s, d = value.shape[:2]
    return value.reshape(s, d, H, C, W).transpose(0, 3, 1, 2, 4)


def matrices(flat):
    k = flat.reshape(2, C, C, 3, 3, 3)
    turned = jnp.flip(k, (3, 4, 5)).transpose(0, 2, 1, 3, 4, 5)
    both = jnp.concatenate([k, turned])
    rows = both.transpose(0, 5, 1, 3, 4, 2)
    rows = jnp.pad(rows, ((0, 0), (0, 0), (0, 0), (0, 0), (2, 2), (0, 0)))
    bands = jnp.stack([rows[:, :, :, :, 3 - h : 7 - h] for h in range(H)], axis=2)
    return bands.reshape(4, 3 * R, 3 * R)


def local(fwd_in, back_out, back_grad, batch_next, loss_grad, weights):
    seg = lax.axis_index("segment")
    slab = lax.axis_index("slab")
    count = lax.axis_size("segment")
    slabs = lax.axis_size("slab")
    ny = slabs // 2
    y, zh = (slab // 2, slab % 2)
    scale = float(fwd_in.shape[3] * slabs * fwd_in.shape[4] * fwd_in.shape[5]) ** (-0.5)

    def route(value, to):
        pairs = []
        for s in range(count):
            for yy in range(ny):
                for zz in range(2):
                    target = to(s, yy, zz)
                    if target is None:
                        continue
                    ts, ty, tz = target
                    if 0 <= ts < count and 0 <= ty < ny:
                        pairs.append((s * slabs + 2 * yy + zz, ts * slabs + 2 * ty + tz))
        return lax.ppermute(value, ("segment", "slab"), pairs)

    def fwd_side(s, zz):
        return 1 - zz if s % SNAKE == SNAKE - 1 and s < count - 1 else zz

    def back_side(s, zz):
        return 1 - zz if s % SNAKE == 0 and s > 0 else zz

    fz = jnp.where((seg % SNAKE == SNAKE - 1) & (seg < count - 1), 1 - zh, zh)
    bz = jnp.where((seg % SNAKE == 0) & (seg > 0), 1 - zh, zh)
    is_first, is_last = (seg == 0, seg == count - 1)

    native = jnp.stack(
        [inside(v[0, k : k + 1])[0] for k, v in ((1, fwd_in), (0, back_out), (1, back_grad), (0, fwd_in), (1, back_out), (0, back_grad))]
    )
    swapped = route(native, lambda s, yy, zz: (s, yy, 1 - zz))

    def rim(value, high):
        return jnp.concatenate([value[:3].reshape(6, R, W), jnp.where(high, value[3:, 1], value[3:, 0])])

    near = route(rim(native, zh == 1), lambda s, yy, zz: (s, yy - 1 + 2 * zz, zz))

    from_first, from_last = (14 % count, (count - 15) % count)
    first_own, last_own = (inside(batch_next), inside(loss_grad[0]))
    ends = jnp.where(seg == from_first, first_own, last_own)

    def end_of(s):
        return 0 if s == from_first else count - 1 if s == from_last else -1

    sp1 = route(ends, lambda s, yy, zz: (end_of(s), yy, 1 - zz))
    sp2 = route(ends, lambda s, yy, zz: (end_of(s), yy + (1 if zz == 1 else -1), 1 - zz))

    mats = matrices(weights[0])
    far = route(rim(swapped, zh == 0), lambda s, yy, zz: (s, yy + 1 - 2 * zz, zz))

    def as_flags(*values):
        return jnp.stack([jnp.asarray(v).astype(jnp.int32) for v in values])

    flags1 = as_flags(zh, y > 0, y < ny - 1, fz, bz)
    fm, fd, bm, bd, ld, y1w, h4, u4, e1p = call(
        tick1_kernel,
        [shaped(8), shaped(2), shaped(16), shaped(4), shaped(2), shaped(6), shaped(4), shaped(4), shaped(2)],
        [planes(8), planes(6), planes(8), planes(6), planes(8), planes(6), planes(4), planes(6), planes(4), planes(6),
         planes(4), planes(8), planes(6)],
        (flags1, mats, native, swapped, near, far),
        3_000_000_000,
    )

    def fwd_diag(s, yy, zz):
        r = fwd_side(s, zz)
        return (s + 1, yy + 1 - 2 * r, r)

    def back_diag(s, yy, zz):
        r = back_side(s, zz)
        return (s - 1, yy + 1 - 2 * r, r)

    bm2 = route(bm, lambda s, yy, zz: (s - 1, yy, back_side(s, zz)))
    bd2 = route(bd, back_diag)
    fm2 = route(fm, lambda s, yy, zz: (s + 1, yy, fwd_side(s, zz)))
    fd2 = route(fd, fwd_diag)
    ld2 = route(ld, lambda s, yy, zz: (s if s == count - 1 else -1, yy + 1 - 2 * zz, zz))
    (dw,) = call(
        wgrad_kernel, [((2, 3 * C, 9 * C), F32)], [], (e1p, u4, native[2], h4), 300_000_000, flagged=False
    )

    flags2 = as_flags(zh, (y > 0) | (zh == 1), (y < ny - 1) | (zh == 0), is_first, is_last)
    out_f, out_b, h4, u4, e1p, d2p = call(
        tick2_kernel,
        [shaped(4), shaped(8), shaped(4), shaped(4), shaped(2), shaped(2)],
        [planes(6), planes(4), planes(6), planes(4), planes(6), planes(4), planes(4), planes(2), planes(4), planes(2),
         planes(4), planes(2), planes(6), planes(4)],
        (flags2, mats, fm2, fd2, bm2, bd2, sp1, sp2, first_own, last_own, y1w, fm, ld2),
        2_000_000_000,
    )
    (dw,) = call(
        functools.partial(wgrad_add_kernel, scale),
        [((2, 3 * C, 9 * C), F32)],
        [],
        (e1p, u4, d2p, h4, dw),
        300_000_000,
        flagged=False,
    )
    back = route(out_b, lambda s, yy, zz: (s - 1, yy, zz))

    parts = dw.reshape(2, 3, C, 9, slabs, C // slabs).transpose(4, 0, 1, 2, 3, 5)
    parts = parts.reshape(slabs, -1, 128)
    parts = lax.all_to_all(parts, "slab", 0, 0, tiled=True)
    total = jnp.sum(parts, axis=0).reshape(2, 3, C, 9, C // slabs)
    total = total.transpose(0, 2, 4, 3, 1).reshape(1, 2, C, -1)

    fwd_out = outside(out_f.reshape(2, 2, R, W))
    back = outside(back.reshape(4, 2, R, W))
    acts = jnp.where(is_last, fwd_out, back[:2])
    grads = jnp.where(is_last, loss_grad[1], back[2:])
    return (fwd_out[None], acts[None], grads[None], total)


def solution(mesh):
    placed = (
        P("segment", None, None, "slab", None, None),
        P("segment", None, None, "slab", None, None),
        P("segment", None, None, "slab", None, None),
        P(None, None, "slab", None, None),
        P(None, None, None, "slab", None, None),
        P("segment", None, None, None),
    )
    return jax.shard_map(
        local,
        mesh=mesh,
        in_specs=placed,
        out_specs=(
            P("segment", None, None, "slab", None, None),
            P("segment", None, None, "slab", None, None),
            P("segment", None, None, "slab", None, None),
            P("segment", None, None, "slab"),
        ),
        check_vma=False,
    )
```

```python
import functools

import jax
import jax.numpy as jnp
import numpy as np
from jax import lax
from jax.experimental import pallas as pl
from jax.experimental.pallas import tpu as pltpu
from jax.sharding import PartitionSpec as P

F32 = jnp.float32
BF16 = jnp.bfloat16
C = 32
H = 4
R = C * H
W = 128
SNAKE = 16


def wide(v):
    return v.astype(F32)


def silu(v):
    v = wide(v)
    return (v / (1.0 + jnp.exp(-v))).astype(BF16)


def slope(v):
    v = wide(v)
    sig = 1.0 / (1.0 + jnp.exp(-v))
    return sig * (1.0 + v * (1.0 - sig))


def conv_planes(w_ref, field, start, count, use):
    lane = lax.broadcasted_iota(jnp.int32, (R, W), 1)
    d = start
    while d < start + count:
        n = min(2, start + count - d)
        x = jnp.concatenate(
            [jnp.concatenate([field[d + k + a] for a in range(3)], axis=0) for k in range(n)], axis=1
        )
        y = jnp.dot(w_ref[...], x, preferred_element_type=F32)
        for k in range(n):
            cols = slice(k * W, (k + 1) * W)
            left = jnp.where(lane >= 1, pltpu.roll(y[:R, cols], 1, 1), 0.0)
            right = jnp.where(lane < W - 1, pltpu.roll(y[2 * R :, cols], W - 1, 1), 0.0)
            use(d + k, y[R : 2 * R, cols] + left + right)
        d += n


def mask(d, v, inner, keep):
    if d == 0:
        v = v * keep[0]
    if d == inner - 1:
        v = v * keep[1]
    return v


def forward(n, keep, w_ref, fb, fa, out_a, out_b, act_b, act_a):
    inner = n - 2
    for p in range(n):
        act_b[p] = silu(fb[p])

    def one(d, v):
        out = mask(d, wide(fa[d]) + v, inner, keep).astype(BF16)
        out_a[d] = out
        act_a[d] = silu(out)

    conv_planes(w_ref.at[0], act_b, 0, inner, one)

    def two(d, v):
        out_b[d] = (wide(fb[d + 2]) + v).astype(BF16)

    conv_planes(w_ref.at[1], act_a, 0, inner - 2, two)


def backward(n, keep, w_ref, bb, ba, db, da, rec_a, rec_b, grad_a, grad_b, act_b, act_a):
    inner = n - 2
    for p in range(n):
        act_b[p] = silu(bb[p])

    def one(d, v):
        out = mask(d, wide(ba[d]) - v, inner, keep).astype(BF16)
        rec_a[d] = out
        act_a[d] = silu(out)

    conv_planes(w_ref.at[1], act_b, 0, inner, one)

    def two(d, v):
        grad_a[d] = mask(d, wide(da[d]) + slope(bb[d + 1]) * v, inner, keep).astype(BF16)

    conv_planes(w_ref.at[3], db, 0, inner, two)

    def three(d, v):
        rec_b[d] = (wide(bb[d + 2]) - v).astype(BF16)

    conv_planes(w_ref.at[0], act_a, 0, inner - 2, three)

    def four(d, v):
        grad_b[d] = (wide(db[d + 2]) + slope(rec_a[d + 1]) * v).astype(BF16)

    conv_planes(w_ref.at[2], grad_a, 0, inner - 2, four)


class Copies:
    def __init__(self, sems):
        self.sems, self.groups, self.n = (sems, [], 0)

    def add(self, pairs, when=None):
        pairs = list(pairs)
        made = [pltpu.make_async_copy(src, dst, self.sems.at[self.n + k]) for k, (src, dst) in enumerate(pairs)]
        self.n += len(made)
        self.groups.append((when, made))

    def each(self, what):
        for when, made in self.groups:
            def run(made=made):
                for copy in made:
                    getattr(copy, what)()

            if when is None:
                run()
            else:
                pl.when(when)(run)

    def start(self):
        self.each("start")

    def wait(self):
        self.each("wait")

    def run(self):
        self.start()
        self.wait()


def at(ref, first, count):
    return ref.at[pl.ds(first, count)]


def window1(zh, b, a, nat_b, nat_a, swp_b, swp_a, near_b, near_a, far_b, far_a):
    return [
        (nat_b, at(b, 2 + 2 * zh, 2)),
        (swp_b, at(b, 4 - 2 * zh, 2)),
        (near_b, at(b, 6 - 6 * zh, 2)),
        (far_b, at(b, 6 * zh, 2)),
        (nat_a, at(a, 1 + 2 * zh, 2)),
        (swp_a, at(a, 3 - 2 * zh, 2)),
        (near_a, at(a, 5 - 5 * zh, 1)),
        (far_a, at(a, 5 * zh, 1)),
    ]


def special(zh, b, a, own, sp1, sp2):
    return [
        (own.at[1], at(b, 2, 2)),
        (sp1.at[1], at(b, 4 - 4 * zh, 2)),
        (sp2.at[1], at(b, 4 * zh, 2)),
        (own.at[0], at(a, 1, 2)),
        (at(sp1.at[0], zh, 1), at(a, 3 - 3 * zh, 1)),
        (at(sp2.at[0], 1 - zh, 1), at(a, 3 * zh, 1)),
    ]


def keeps(flags):
    return (flags[1].astype(F32), flags[2].astype(F32))


def tick1_back(flags, w_ref, nat, swp, near, far, bm, bd, h4, u4, e1p, *scratch):
    bb, ba, db, da, rec_a, rec_b, grad_a, grad_b, act_b, act_a, sems = scratch
    zh, bz = (flags[0], flags[4])
    load = Copies(sems)
    for k, (b, a) in enumerate(((bb, ba), (db, da))):
        load.add(
            window1(
                zh, b, a, nat.at[k], nat.at[2 + k], swp.at[k], swp.at[2 + k],
                at(near, 2 * k, 2), at(near, 4 + k, 1), at(far, 2 * k, 2), at(far, 4 + k, 1),
            )
        )
    load.run()
    backward(8, keeps(flags), w_ref, bb, ba, db, da, rec_a, rec_b, grad_a, grad_b, act_b, act_a)
    save = Copies(sems)
    save.add([
        (rec_b, at(bm, 0, 4)),
        (grad_b, at(bm, 4, 4)),
        (at(rec_a, 2 * bz, 4), at(bm, 8, 4)),
        (at(grad_a, 2 * bz, 4), at(bm, 12, 4)),
        (at(rec_b, 2 - 2 * bz, 2), at(bd, 0, 2)),
        (at(grad_b, 2 - 2 * bz, 2), at(bd, 2, 2)),
        (at(act_b, 1 + 2 * zh, 4), h4),
        (at(act_a, 2 * zh, 4), u4),
        (at(grad_a, 1 + 2 * zh, 2), e1p),
    ])
    save.run()


def tick1_forward(flags, w_ref, nat, swp, near, far, fm, fd, ld, y1w, *scratch):
    fb, fa, out_a, out_b, act_b, act_a, sems = scratch
    zh, fz = (flags[0], flags[3])
    load = Copies(sems)
    load.add(
        window1(
            zh, fb, fa, nat.at[0], nat.at[1], swp.at[0], swp.at[1],
            at(near, 6, 2), at(near, 8, 1), at(far, 0, 2), at(far, 2, 1),
        )
    )
    load.run()
    forward(8, keeps(flags), w_ref, fb, fa, out_a, out_b, act_b, act_a)
    save = Copies(sems)
    save.add([
        (out_b, at(fm, 0, 4)),
        (at(out_a, 2 * fz, 4), at(fm, 4, 4)),
        (at(out_b, 2 - 2 * fz, 2), fd),
        (at(out_a, 3 - zh, 1), at(ld, zh, 1)),
        (at(out_b, 3 - 3 * zh, 1), at(ld, 1 - zh, 1)),
        (out_a, y1w),
    ])
    save.run()


def tick2_back(
    scale, flags, w_ref, order, bm, bd, sp1, sp2, last_own, y1w, own, ld, dw, out, parts, *scratch
):
    bb, ba, db, da, rec_a, rec_b, grad_a, grad_b, act_b, act_a, sems = scratch
    zh, last = (flags[0], flags[4] == 1)
    main, halo = (2 - 2 * zh, 4 * zh)
    load = Copies(sems)
    load.add(
        special(zh, db, da, last_own, sp1, sp2)
        + [
            (at(y1w, zh, 5), at(bb, 1 - zh, 5)),
            (at(ld, zh, 1), at(bb, 5 * zh, 1)),
            (at(own, zh, 3), at(ba, 1 - zh, 3)),
            (at(ld, 1 - zh, 1), at(ba, 3 * zh, 1)),
        ],
        last,
    )
    load.add(
        [
            (at(bm, 0, 4), at(bb, main, 4)),
            (at(bd, 0, 2), at(bb, halo, 2)),
            (at(bm, 4, 4), at(db, main, 4)),
            (at(bd, 2, 2), at(db, halo, 2)),
            (at(bm, 8, 4), ba),
            (at(bm, 12, 4), da),
        ],
        flags[4] == 0,
    )
    load.run()
    backward(6, keeps(flags), w_ref, bb, ba, db, da, rec_a, rec_b, grad_a, grad_b, act_b, act_a)
    save = Copies(sems)
    save.add([
        (rec_b, at(out, 0, 2)),
        (at(rec_a, 1, 2), at(out, 2, 2)),
        (at(grad_a, 1, 2), at(out, 4, 2)),
        (grad_b, at(out, 6, 2)),
    ])
    save.start()
    sums = [
        dw[0] + wgrad_pair(at(grad_a, 1, 2), act_a),
        dw[1] + wgrad_pair(at(db, 2, 2), at(act_b, 1, 4)),
    ]
    sums = jnp.concatenate([(v * scale).astype(BF16) for v in sums], axis=0)
    ordered = jnp.dot(order[...], sums, preferred_element_type=F32).astype(BF16)
    parts[:, :, : 3 * C] = ordered.reshape(*parts.shape[:2], 3 * C)
    parts[:, :, 3 * C :] = jnp.zeros((*parts.shape[:2], W - 3 * C), BF16)
    save.wait()


def tick2_forward(flags, w_ref, fm, fd, sp1, sp2, first_own, out, *scratch):
    fb, fa, out_a, out_b, act_b, act_a, sems = scratch
    zh, first = (flags[0], flags[3])
    main, halo = (2 - 2 * zh, 4 * zh)
    load = Copies(sems)
    load.add(special(zh, fb, fa, first_own, sp1, sp2), first == 1)
    load.add(
        [(at(fm, 0, 4), at(fb, main, 4)), (fd, at(fb, halo, 2)), (at(fm, 4, 4), fa)],
        first == 0,
    )
    load.run()
    forward(6, keeps(flags), w_ref, fb, fa, out_a, out_b, act_b, act_a)
    out[0] = out_a[1]
    out[1] = out_a[2]
    out[2] = out_b[0]
    out[3] = out_b[1]


def wgrad_pair(g_ref, u_ref):
    lane = lax.broadcasted_iota(jnp.int32, (C, W), 1)
    zero = jnp.zeros((C, W), BF16)
    left, right = ([], [])
    for d in range(2):
        for h in range(H):
            g = wide(g_ref[d, h * C : (h + 1) * C])
            down = jnp.where(lane < W - 1, pltpu.roll(g, W - 1, 1), 0.0)
            up = jnp.where(lane >= 1, pltpu.roll(g, 1, 1), 0.0)
            left.append(jnp.concatenate([down, g, up], axis=0).astype(BF16))
            rows = []
            for a in range(3):
                for b in range(3):
                    at = h + b - 1
                    rows.append(u_ref[d + a, at * C : (at + 1) * C] if 0 <= at < H else zero)
            right.append(jnp.concatenate(rows, axis=0))
    return lax.dot_general(
        jnp.concatenate(right, axis=1),
        jnp.concatenate(left, axis=1),
        (((1,), (1,)), ((), ())),
        preferred_element_type=F32,
    )


def wgrad_kernel(e1, u4, d2, h4, out):
    out[0] = wgrad_pair(e1, u4)
    out[1] = wgrad_pair(d2, h4)


def bands_kernel(rows, out):
    lane = lax.broadcasted_iota(jnp.int32, (C, R), 1)
    for kind in range(4):
        for c in range(3):
            for a in range(3):
                tile = wide(rows[kind, c, :, a * R : (a + 1) * R])
                for h in range(H):
                    moved = tile if h == 1 else pltpu.roll(tile, ((h - 1) * C) % R, 1)
                    if h == 0:
                        moved = jnp.where(lane < 2 * C, moved, 0.0)
                    if h == 3:
                        moved = jnp.where(lane >= 2 * C, moved, 0.0)
                    at_row = (c * H + h) * C
                    out[kind, at_row : at_row + C, a * R : (a + 1) * R] = moved.astype(BF16)


VMEM = pl.BlockSpec(memory_space=pltpu.VMEM)
SMEM = pl.BlockSpec(memory_space=pltpu.SMEM)
HBM = pl.BlockSpec(memory_space=pltpu.HBM)


def call(kernel, outs, scratch, args, flops, specs, out_specs):
    return pl.pallas_call(
        kernel,
        out_shape=tuple(jax.ShapeDtypeStruct(s, t) for s, t in outs),
        in_specs=specs,
        out_specs=tuple(out_specs),
        scratch_shapes=scratch,
        compiler_params=pltpu.CompilerParams(vmem_limit_bytes=40 * 2**20),
        cost_estimate=pl.CostEstimate(flops=flops, bytes_accessed=4_000_000, transcendentals=400_000),
    )(*args)


def order_rows(slabs):
    per = C // slabs
    used = 2 * 9 * per
    rows = -(-used // 16) * 16
    out = np.zeros((slabs, rows, 2, 9, C), np.float32)
    for j in range(slabs):
        for p in range(2):
            for ab in range(9):
                for k in range(per):
                    out[j, (p * 9 + ab) * per + k, p, ab, j * per + k] = 1
    return jnp.asarray(out.reshape(slabs * rows, -1), BF16), rows


def planes(*lead):
    return pltpu.VMEM((*lead, R, W), BF16)


def shaped(*lead):
    return ((*lead, R, W), BF16)


def inside(value):
    s, _, d = value.shape[:3]
    return value.transpose(0, 2, 3, 1, 4).reshape(s, d, R, W)


def outside(value):
    s, d = value.shape[:2]
    return value.reshape(s, d, H, C, W).transpose(0, 3, 1, 2, 4)


def matrices(flat):
    k = flat.reshape(2, C, C, 3, 3, 3)
    turned = jnp.flip(k, (3, 4, 5)).transpose(0, 2, 1, 3, 4, 5)
    both = jnp.concatenate([k, turned])
    rows = both.transpose(0, 5, 1, 3, 4, 2)
    rows = jnp.pad(rows, ((0, 0), (0, 0), (0, 0), (0, 0), (0, 1), (0, 0))).reshape(4, 3, C, 3 * R)
    (out,) = call(bands_kernel, [((4, 3 * R, 3 * R), BF16)], [], (rows,), 1_000_000, [VMEM], [VMEM])
    return out


def local(fwd_in, back_out, back_grad, batch_next, loss_grad, weights):
    seg = lax.axis_index("segment")
    slab = lax.axis_index("slab")
    count = lax.axis_size("segment")
    slabs = lax.axis_size("slab")
    ny = slabs // 2
    y, zh = (slab // 2, slab % 2)
    scale = float(fwd_in.shape[3] * slabs * fwd_in.shape[4] * fwd_in.shape[5]) ** (-0.5)

    def route(value, to):
        pairs = []
        for s in range(count):
            for yy in range(ny):
                for zz in range(2):
                    target = to(s, yy, zz)
                    if target is None:
                        continue
                    ts, ty, tz = target
                    if 0 <= ts < count and 0 <= ty < ny:
                        pairs.append((s * slabs + 2 * yy + zz, ts * slabs + 2 * ty + tz))
        return lax.ppermute(value, ("segment", "slab"), pairs)

    def fwd_side(s, zz):
        return 1 - zz if s % SNAKE == SNAKE - 1 and s < count - 1 else zz

    def back_side(s, zz):
        return 1 - zz if s % SNAKE == 0 and s > 0 else zz

    fz = jnp.where((seg % SNAKE == SNAKE - 1) & (seg < count - 1), 1 - zh, zh)
    bz = jnp.where((seg % SNAKE == 0) & (seg > 0), 1 - zh, zh)
    is_first, is_last = (seg == 0, seg == count - 1)

    def swap(value):
        return route(value, lambda s, yy, zz: (s, yy, 1 - zz))

    def rim(value, high):
        n = value.shape[0] // 2
        return jnp.concatenate([value[:n].reshape(2 * n, R, W), jnp.where(high, value[n:, 1], value[n:, 0])])

    nat_b = jnp.stack([inside(v[0, k : k + 1])[0] for k, v in ((0, back_out), (1, back_grad), (1, back_out), (0, back_grad))])
    swp_b = swap(nat_b)
    nat_f = inside(fwd_in[0])[::-1]
    swp_f = swap(nat_f)
    near = route(
        jnp.concatenate([rim(nat_b, zh == 1), rim(nat_f, zh == 1)]), lambda s, yy, zz: (s, yy - 1 + 2 * zz, zz)
    )

    from_first, from_last = (14 % count, (count - 15) % count)
    first_own, last_own = (inside(batch_next), inside(loss_grad[0]))
    ends = jnp.where(seg == from_first, first_own, last_own)

    def end_of(s):
        return 0 if s == from_first else count - 1 if s == from_last else -1

    sp1 = route(ends, lambda s, yy, zz: (end_of(s), yy, 1 - zz))
    sp2 = route(ends, lambda s, yy, zz: (end_of(s), yy + (1 if zz == 1 else -1), 1 - zz))
    mats = matrices(weights[0])

    def as_flags(*values):
        return jnp.stack([jnp.asarray(v).astype(jnp.int32) for v in values])

    flags1 = as_flags(zh, y > 0, y < ny - 1, fz, bz)
    flags2 = as_flags(zh, (y > 0) | (zh == 1), (y < ny - 1) | (zh == 0), is_first, is_last)
    order, rows = order_rows(slabs)

    swp_b, near, sp1, sp2, mats = lax.optimization_barrier((swp_b, near, sp1, sp2, mats))

    def onward(value):
        return route(rim(value, zh == 0), lambda s, yy, zz: (s, yy + 1 - 2 * zz, zz))

    far_b = onward(swp_b)
    sems = pltpu.SemaphoreType.DMA((20,))
    bm, bd, h4, u4, e1p = call(
        tick1_back,
        [shaped(16), shaped(4), shaped(4), shaped(4), shaped(2)],
        [planes(8), planes(6), planes(8), planes(6), planes(6), planes(4), planes(6), planes(4), planes(8), planes(6), sems],
        (flags1, mats, nat_b, swp_b, near, far_b),
        2_000_000_000,
        [SMEM, VMEM] + [HBM] * 4,
        [HBM] * 5,
    )

    def fwd_diag(s, yy, zz):
        r = fwd_side(s, zz)
        return (s + 1, yy + 1 - 2 * r, r)

    def back_diag(s, yy, zz):
        r = back_side(s, zz)
        return (s - 1, yy + 1 - 2 * r, r)

    bm2 = route(bm, lambda s, yy, zz: (s - 1, yy, back_side(s, zz)))
    bd2 = route(bd, back_diag)
    (dw,) = call(
        wgrad_kernel, [((2, 9 * C, 3 * C), F32)], [], (e1p, u4, nat_b[1], h4), 300_000_000, [VMEM] * 4, [VMEM]
    )

    swp_f, bm = lax.optimization_barrier((swp_f, bm))
    far_f = onward(swp_f)
    fm, fd, ld, y1w = call(
        tick1_forward,
        [shaped(8), shaped(2), shaped(2), shaped(6)],
        [planes(8), planes(6), planes(6), planes(4), planes(8), planes(6), sems],
        (flags1, mats, nat_f, swp_f, near, far_f),
        1_000_000_000,
        [SMEM, VMEM] + [HBM] * 4,
        [HBM] * 4,
    )
    ld2 = route(ld, lambda s, yy, zz: (s if s == count - 1 else -1, yy + 1 - 2 * zz, zz))
    fd2 = route(fd, fwd_diag)
    fm2 = route(fm, lambda s, yy, zz: (s + 1, yy, fwd_side(s, zz)))

    out_b, parts = call(
        functools.partial(tick2_back, scale),
        [shaped(8), ((slabs, rows, W), BF16)],
        [planes(6), planes(4), planes(6), planes(4), planes(4), planes(2), planes(4), planes(2), planes(6), planes(4), sems],
        (flags2, mats, order, bm2, bd2, sp1, sp2, last_own, y1w, fm, ld2, dw),
        1_500_000_000,
        [SMEM, VMEM, VMEM] + [HBM] * 8 + [VMEM],
        [HBM, VMEM],
    )
    back = route(out_b, lambda s, yy, zz: (s - 1, yy, zz))
    parts = lax.all_to_all(parts, "slab", 0, 0, tiled=True)

    fm2, out_b = lax.optimization_barrier((fm2, out_b))
    (out_f,) = call(
        tick2_forward,
        [shaped(4)],
        [planes(6), planes(4), planes(4), planes(2), planes(6), planes(4), sems],
        (flags2, mats, fm2, fd2, sp1, sp2, first_own),
        700_000_000,
        [SMEM, VMEM] + [HBM] * 5,
        [VMEM],
    )

    total = jnp.sum(wide(parts), axis=0)[: 2 * 9 * (C // slabs), : 3 * C]
    total = total.reshape(2, 9, C // slabs, 3, C).transpose(0, 4, 2, 1, 3).reshape(1, 2, C, -1)

    fwd_out = outside(out_f.reshape(2, 2, R, W))
    back = outside(back.reshape(4, 2, R, W))
    acts = jnp.where(is_last, fwd_out, back[:2])
    grads = jnp.where(is_last, loss_grad[1], back[2:])
    return (fwd_out[None], acts[None], grads[None], total)


def solution(mesh):
    placed = (
        P("segment", None, None, "slab", None, None),
        P("segment", None, None, "slab", None, None),
        P("segment", None, None, "slab", None, None),
        P(None, None, "slab", None, None),
        P(None, None, None, "slab", None, None),
        P("segment", None, None, None),
    )
    return jax.shard_map(
        local,
        mesh=mesh,
        in_specs=placed,
        out_specs=(
            P("segment", None, None, "slab", None, None),
            P("segment", None, None, "slab", None, None),
            P("segment", None, None, "slab", None, None),
            P("segment", None, None, "slab"),
        ),
        check_vma=False,
    )
```

```python
import functools

import jax
import jax.numpy as jnp
from jax import lax
from jax.experimental import pallas as pl
from jax.experimental.pallas import tpu as pltpu
from jax.sharding import PartitionSpec as P

F32 = jnp.float32
BF16 = jnp.bfloat16
C = 32
H = 4
R = C * H
W = 128
SNAKE = 16


def wide(v):
    return v.astype(F32)


def silu(v):
    v = wide(v)
    return (v / (1.0 + jnp.exp(-v))).astype(BF16)


def slope(v):
    v = wide(v)
    sig = 1.0 / (1.0 + jnp.exp(-v))
    return sig * (1.0 + v * (1.0 - sig))


def conv_planes(w_ref, field, start, count, use):
    lane = lax.broadcasted_iota(jnp.int32, (R, W), 1)
    d = start
    while d < start + count:
        n = min(2, start + count - d)
        x = jnp.concatenate(
            [jnp.concatenate([field[d + k + a] for a in range(3)], axis=0) for k in range(n)], axis=1
        )
        y = jnp.dot(w_ref[...], x, preferred_element_type=F32)
        for k in range(n):
            cols = slice(k * W, (k + 1) * W)
            left = jnp.where(lane >= 1, pltpu.roll(y[:R, cols], 1, 1), 0.0)
            right = jnp.where(lane < W - 1, pltpu.roll(y[2 * R :, cols], W - 1, 1), 0.0)
            use(d + k, y[R : 2 * R, cols] + left + right)
        d += n


def mask(d, v, inner, keep):
    if d == 0:
        v = v * keep[0]
    if d == inner - 1:
        v = v * keep[1]
    return v


def forward(n, keep, w_ref, fb, fa, out_a, out_b, act_b, act_a):
    inner = n - 2
    for p in range(n):
        act_b[p] = silu(fb[p])

    def one(d, v):
        out = mask(d, wide(fa[d]) + v, inner, keep).astype(BF16)
        out_a[d] = out
        act_a[d] = silu(out)

    conv_planes(w_ref.at[0], act_b, 0, inner, one)

    def two(d, v):
        out_b[d] = (wide(fb[d + 2]) + v).astype(BF16)

    conv_planes(w_ref.at[1], act_a, 0, inner - 2, two)


def backward(n, keep, w_ref, bb, ba, db, da, rec_a, rec_b, grad_a, grad_b, act_b, act_a):
    inner = n - 2
    for p in range(n):
        act_b[p] = silu(bb[p])

    def one(d, v):
        out = mask(d, wide(ba[d]) - v, inner, keep).astype(BF16)
        rec_a[d] = out
        act_a[d] = silu(out)

    conv_planes(w_ref.at[1], act_b, 0, inner, one)

    def two(d, v):
        grad_a[d] = mask(d, wide(da[d]) + slope(bb[d + 1]) * v, inner, keep).astype(BF16)

    conv_planes(w_ref.at[3], db, 0, inner, two)

    def three(d, v):
        rec_b[d] = (wide(bb[d + 2]) - v).astype(BF16)

    conv_planes(w_ref.at[0], act_a, 0, inner - 2, three)

    def four(d, v):
        grad_b[d] = (wide(db[d + 2]) + slope(rec_a[d + 1]) * v).astype(BF16)

    conv_planes(w_ref.at[2], grad_a, 0, inner - 2, four)


class Copies:
    def __init__(self, sems):
        self.sems, self.groups, self.n = (sems, [], 0)

    def add(self, pairs, when=None):
        pairs = list(pairs)
        made = [pltpu.make_async_copy(src, dst, self.sems.at[self.n + k]) for k, (src, dst) in enumerate(pairs)]
        self.n += len(made)
        self.groups.append((when, made))

    def each(self, what):
        for when, made in self.groups:
            def run(made=made):
                for copy in made:
                    getattr(copy, what)()

            if when is None:
                run()
            else:
                pl.when(when)(run)

    def start(self):
        self.each("start")

    def wait(self):
        self.each("wait")

    def run(self):
        self.start()
        self.wait()


def at(ref, first, count):
    return ref.at[pl.ds(first, count)]


def window1(zh, b, a, nat_b, nat_a, swp_b, swp_a, near_b, near_a, far_b, far_a):
    return [
        (nat_b, at(b, 2 + 2 * zh, 2)),
        (swp_b, at(b, 4 - 2 * zh, 2)),
        (near_b, at(b, 6 - 6 * zh, 2)),
        (far_b, at(b, 6 * zh, 2)),
        (nat_a, at(a, 1 + 2 * zh, 2)),
        (swp_a, at(a, 3 - 2 * zh, 2)),
        (near_a, at(a, 5 - 5 * zh, 1)),
        (far_a, at(a, 5 * zh, 1)),
    ]


def special(zh, b, a, own, sp1, sp2):
    return [
        (own[1], at(b, 2, 2)),
        (sp1.at[1], at(b, 4 - 4 * zh, 2)),
        (sp2.at[1], at(b, 4 * zh, 2)),
        (own[0], at(a, 1, 2)),
        (at(sp1.at[0], zh, 1), at(a, 3 - 3 * zh, 1)),
        (at(sp2.at[0], 1 - zh, 1), at(a, 3 * zh, 1)),
    ]


def keeps(flags):
    return (flags[1].astype(F32), flags[2].astype(F32))


def tick1_back(flags, w_ref, nat, swp, near, far, bm, bd, dw, *scratch):
    bb, ba, db, da, rec_a, rec_b, grad_a, grad_b, act_b, act_a, sems = scratch
    zh, bz = (flags[0], flags[4])
    load = Copies(sems)
    for k, (b, a) in enumerate(((bb, ba), (db, da))):
        load.add(
            window1(
                zh, b, a, at(nat, 2 * k, 2), at(nat, 4 + 2 * k, 2), at(swp, 2 * k, 2), at(swp, 4 + 2 * k, 2),
                at(near, 2 * k, 2), at(near, 4 + k, 1), at(far, 2 * k, 2), at(far, 5 + 2 * k - zh, 1),
            )
        )
    load.run()
    backward(8, keeps(flags), w_ref, bb, ba, db, da, rec_a, rec_b, grad_a, grad_b, act_b, act_a)
    save = Copies(sems)
    save.add([
        (rec_b, at(bm, 0, 4)),
        (grad_b, at(bm, 4, 4)),
        (at(rec_a, 2 * bz, 4), at(bm, 8, 4)),
        (at(grad_a, 2 * bz, 4), at(bm, 12, 4)),
        (at(rec_b, 2 - 2 * bz, 2), at(bd, 0, 2)),
        (at(grad_b, 2 - 2 * bz, 2), at(bd, 2, 2)),
    ])
    save.start()
    dw[0] = wgrad_pair(at(grad_a, 1 + 2 * zh, 2), at(act_a, 2 * zh, 4))
    dw[1] = wgrad_pair(at(db, 2 + 2 * zh, 2), at(act_b, 1 + 2 * zh, 4))
    save.wait()


def tick1_forward(flags, w_ref, nat, swp, near, far, last_own, fm, fd, ld, y1w, *scratch):
    fb, fa, out_a, out_b, act_b, act_a, sems = scratch
    zh, fz = (flags[0], flags[3])
    load = Copies(sems)
    load.add(
        window1(
            zh, fb, fa, at(nat, 0, 2), at(nat, 2, 2), at(swp, 0, 2), at(swp, 2, 2),
            at(near, 6, 2), at(near, 8, 1), at(far, 0, 2), at(far, 3 - zh, 1),
        )
    )
    load.run()
    forward(8, keeps(flags), w_ref, fb, fa, out_a, out_b, act_b, act_a)
    save = Copies(sems)
    save.add([
        (out_b, at(fm, 0, 4)),
        (at(out_a, 2 * fz, 4), at(fm, 4, 4)),
        (at(out_b, 2 - 2 * fz, 2), fd),
        (at(out_a, 3 - zh, 1), at(ld, zh, 1)),
        (at(out_b, 3 - 3 * zh, 1), at(ld, 1 - zh, 1)),
        (out_a, at(y1w, 0, 6)),
        (last_own.at[0], at(y1w, 6, 2)),
        (last_own.at[1], at(y1w, 8, 2)),
    ])
    save.run()


def tick2_back(
    scale, flags, w_ref, bm, bd, sp1, sp2, y1w, own, ld, dw, out, parts, *scratch
):
    bb, ba, db, da, rec_a, rec_b, grad_a, grad_b, act_b, act_a, sems = scratch
    zh, last = (flags[0], flags[4] == 1)
    main, halo = (2 - 2 * zh, 4 * zh)
    load = Copies(sems)
    load.add(
        special(zh, db, da, (at(y1w, 6, 2), at(y1w, 8, 2)), sp1, sp2)
        + [
            (at(y1w, zh, 5), at(bb, 1 - zh, 5)),
            (at(ld, zh, 1), at(bb, 5 * zh, 1)),
            (at(own, zh, 3), at(ba, 1 - zh, 3)),
            (at(ld, 1 - zh, 1), at(ba, 3 * zh, 1)),
        ],
        last,
    )
    load.add(
        [
            (at(bm, 0, 4), at(bb, main, 4)),
            (at(bd, 0, 2), at(bb, halo, 2)),
            (at(bm, 4, 4), at(db, main, 4)),
            (at(bd, 2, 2), at(db, halo, 2)),
            (at(bm, 8, 4), ba),
            (at(bm, 12, 4), da),
        ],
        flags[4] == 0,
    )
    load.start()
    order, back_order = (slab_order(parts.shape[0]), to_outside())
    load.wait()
    backward(6, keeps(flags), w_ref, bb, ba, db, da, rec_a, rec_b, grad_a, grad_b, act_b, act_a)
    pieces = [rec_b[...], rec_a[1:3], grad_a[1:3], grad_b[...]]
    for k, v in enumerate(reorder(back_order, [p.reshape(2 * R, W) for p in pieces])):
        out[k] = v
    sums = [
        dw[0] + wgrad_pair(at(grad_a, 1, 2), act_a),
        dw[1] + wgrad_pair(at(db, 2, 2), at(act_b, 1, 4)),
    ]
    sums = jnp.concatenate([(v * scale).astype(BF16) for v in sums], axis=0)
    ordered = jnp.dot(order, sums, preferred_element_type=F32).astype(BF16)
    parts[:, :, : 3 * C] = ordered.reshape(*parts.shape[:2], 3 * C)
    parts[:, :, 3 * C :] = jnp.zeros((*parts.shape[:2], W - 3 * C), BF16)


def tick2_forward(flags, w_ref, fm, fd, sp1, sp2, first_own, out, *scratch):
    fb, fa, out_a, out_b, act_b, act_a, sems = scratch
    zh, first = (flags[0], flags[3])
    main, halo = (2 - 2 * zh, 4 * zh)
    load = Copies(sems)
    load.add(special(zh, fb, fa, (first_own.at[0], first_own.at[1]), sp1, sp2), first == 1)
    load.add(
        [(at(fm, 0, 4), at(fb, main, 4)), (fd, at(fb, halo, 2)), (at(fm, 4, 4), fa)],
        first == 0,
    )
    load.run()
    forward(6, keeps(flags), w_ref, fb, fa, out_a, out_b, act_b, act_a)
    for k, v in enumerate(reorder(to_outside(), [p.reshape(2 * R, W) for p in (out_a[1:3], out_b[...])])):
        out[k] = v


def wgrad_pair(g_ref, u_ref):
    lane = lax.broadcasted_iota(jnp.int32, (C, W), 1)
    zero = jnp.zeros((C, W), BF16)
    left, right = ([], [])
    for d in range(2):
        for h in range(H):
            g = wide(g_ref[d, h * C : (h + 1) * C])
            down = jnp.where(lane < W - 1, pltpu.roll(g, W - 1, 1), 0.0)
            up = jnp.where(lane >= 1, pltpu.roll(g, 1, 1), 0.0)
            left.append(jnp.concatenate([down, g, up], axis=0).astype(BF16))
            rows = []
            for a in range(3):
                for b in range(3):
                    at = h + b - 1
                    rows.append(u_ref[d + a, at * C : (at + 1) * C] if 0 <= at < H else zero)
            right.append(jnp.concatenate(rows, axis=0))
    return lax.dot_general(
        jnp.concatenate(right, axis=1),
        jnp.concatenate(left, axis=1),
        (((1,), (1,)), ((), ())),
        preferred_element_type=F32,
    )


def bands_kernel(rows, out):
    lane = lax.broadcasted_iota(jnp.int32, (C, R), 1)
    for kind in range(4):
        for c in range(3):
            for a in range(3):
                tile = wide(rows[kind, c, :, a * R : (a + 1) * R])
                for h in range(H):
                    moved = tile if h == 1 else pltpu.roll(tile, ((h - 1) * C) % R, 1)
                    if h == 0:
                        moved = jnp.where(lane < 2 * C, moved, 0.0)
                    if h == 3:
                        moved = jnp.where(lane >= 2 * C, moved, 0.0)
                    at_row = (c * H + h) * C
                    out[kind, at_row : at_row + C, a * R : (a + 1) * R] = moved.astype(BF16)


VMEM = pl.BlockSpec(memory_space=pltpu.VMEM)
SMEM = pl.BlockSpec(memory_space=pltpu.SMEM)
HBM = pl.BlockSpec(memory_space=pltpu.HBM)


def call(kernel, outs, scratch, args, flops, specs, out_specs, mib=16):
    return pl.pallas_call(
        kernel,
        out_shape=tuple(jax.ShapeDtypeStruct(s, t) for s, t in outs),
        in_specs=specs,
        out_specs=tuple(out_specs),
        scratch_shapes=scratch,
        compiler_params=pltpu.CompilerParams(vmem_limit_bytes=mib * 2**20),
        cost_estimate=pl.CostEstimate(flops=flops, bytes_accessed=4_000_000, transcendentals=400_000),
    )(*args)


def slab_rows(slabs):
    return -(-2 * 9 * C // (16 * slabs)) * 16


def slab_order(slabs):
    per = C // slabs
    low, rows = (per.bit_length() - 1, slab_rows(slabs))
    return one_hot(
        slabs * rows, 2 * 9 * C, lambda n: ((n & (C - 1)) >> low) * rows + (n >> 5) * per + (n & (per - 1))
    )


def planes(*lead):
    return pltpu.VMEM((*lead, R, W), BF16)


def shaped(*lead):
    return ((*lead, R, W), BF16)


def flat_rows(value):
    return value.reshape(value.shape[0], -1, W)


def one_hot(rows, cols, target):
    row = lax.broadcasted_iota(jnp.int32, (rows, cols), 0)
    col = lax.broadcasted_iota(jnp.int32, (rows, cols), 1)
    return jnp.where(row == target(col), 1.0, 0.0).astype(BF16)


def to_inside():
    return one_hot(2 * R, 2 * R, lambda n: (n & 7) * C + (n >> 3))


def to_outside():
    return one_hot(2 * R, 2 * R, lambda n: (n & (C - 1)) * 8 + (n >> 5))


def reorder(matrix, pieces):
    both = jnp.dot(matrix, jnp.concatenate(pieces, axis=1), preferred_element_type=F32).astype(BF16)
    return [both[:, k * W : (k + 1) * W] for k in range(len(pieces))]


def prepare_kernel(flags, fwd_hbm, acts_hbm, grads_hbm, nat_b, nat_f, near, fwd, acts, grads, sems):
    zh = flags[0]
    load = Copies(sems)
    load.add([(fwd_hbm, fwd), (acts_hbm, acts), (grads_hbm, grads)])
    load.start()
    order = to_inside()
    load.wait()
    streams = reorder(order, [acts[0], grads[1], acts[1], grads[0], fwd[1], fwd[0]])
    for k, v in enumerate(streams):
        ref, at_k = (nat_b, k) if k < 4 else (nat_f, k - 4)
        ref[2 * at_k] = v[:R]
        ref[2 * at_k + 1] = v[R:]
    for k, src in ((0, 0), (2, 1), (6, 4)):
        near[k] = streams[src][:R]
        near[k + 1] = streams[src][R:]
    for k, ref, src in ((4, nat_b, 4), (5, nat_b, 6), (8, nat_f, 2)):
        near[k] = ref[src + zh]


def prepare_ends_kernel(flags, batch, loss, first_own, last_own, ends):
    x1, x2, d1, d2 = reorder(to_inside(), [batch[0], batch[1], loss[0], loss[1]])
    for ref, pair in ((first_own, (x1, x2)), (last_own, (d1, d2))):
        for k in range(2):
            ref[k, 0] = pair[k][:R]
            ref[k, 1] = pair[k][R:]
    first = flags[5] == 1

    @pl.when(first)
    def _():
        ends[...] = first_own[...]

    @pl.when(jnp.logical_not(first))
    def _():
        ends[...] = last_own[...]


def matrices(flat):
    k = flat.reshape(2, C, C, 3, 3, 3)
    turned = jnp.flip(k, (3, 4, 5)).transpose(0, 2, 1, 3, 4, 5)
    both = jnp.concatenate([k, turned])
    rows = both.transpose(0, 5, 1, 3, 4, 2)
    rows = jnp.pad(rows, ((0, 0), (0, 0), (0, 0), (0, 0), (0, 1), (0, 0))).reshape(4, 3, C, 3 * R)
    (out,) = call(bands_kernel, [((4, 3 * R, 3 * R), BF16)], [], (rows,), 1_000_000, [VMEM], [VMEM])
    return out


def local(fwd_in, back_out, back_grad, batch_next, loss_grad, weights):
    seg = lax.axis_index("segment")
    slab = lax.axis_index("slab")
    count = lax.axis_size("segment")
    slabs = lax.axis_size("slab")
    ny = slabs // 2
    y, zh = (slab // 2, slab % 2)
    scale = float(fwd_in.shape[3] * slabs * fwd_in.shape[4] * fwd_in.shape[5]) ** (-0.5)

    def route(value, to):
        pairs = []
        for s in range(count):
            for yy in range(ny):
                for zz in range(2):
                    target = to(s, yy, zz)
                    if target is None:
                        continue
                    ts, ty, tz = target
                    if 0 <= ts < count and 0 <= ty < ny:
                        pairs.append((s * slabs + 2 * yy + zz, ts * slabs + 2 * ty + tz))
        return lax.ppermute(value, ("segment", "slab"), pairs)

    def fwd_side(s, zz):
        return 1 - zz if s % SNAKE == SNAKE - 1 and s < count - 1 else zz

    def back_side(s, zz):
        return 1 - zz if s % SNAKE == 0 and s > 0 else zz

    fz = jnp.where((seg % SNAKE == SNAKE - 1) & (seg < count - 1), 1 - zh, zh)
    bz = jnp.where((seg % SNAKE == 0) & (seg > 0), 1 - zh, zh)
    is_first, is_last = (seg == 0, seg == count - 1)

    def swap(value):
        return route(value, lambda s, yy, zz: (s, yy, 1 - zz))

    def as_flags(*values):
        return jnp.stack([jnp.asarray(v).astype(jnp.int32) for v in values])

    from_first, from_last = (14 % count, (count - 15) % count)
    flags1 = as_flags(zh, y > 0, y < ny - 1, fz, bz, seg == from_first)
    flags2 = as_flags(zh, (y > 0) | (zh == 1), (y < ny - 1) | (zh == 0), is_first, is_last)
    nat_b, nat_f, near = call(
        prepare_kernel,
        [shaped(8), shaped(4), shaped(9)],
        [pltpu.VMEM((2, 2 * R, W), BF16)] * 3 + [pltpu.SemaphoreType.DMA((3,))],
        (flags1, flat_rows(fwd_in[0]), flat_rows(back_out[0]), flat_rows(back_grad[0])),
        100_000_000,
        [SMEM] + [HBM] * 3,
        [VMEM] * 3,
        58,
    )
    swp_b = swap(nat_b)
    swp_f = swap(nat_f)
    near = route(near, lambda s, yy, zz: (s, yy - 1 + 2 * zz, zz))
    first_own, last_own, ends = call(
        prepare_ends_kernel,
        [shaped(2, 2)] * 3,
        [],
        (flags1, flat_rows(batch_next), flat_rows(loss_grad[0])),
        100_000_000,
        [SMEM] + [VMEM] * 2,
        [VMEM] * 3,
    )

    def end_of(s):
        return 0 if s == from_first else count - 1 if s == from_last else -1

    sp1 = route(ends, lambda s, yy, zz: (end_of(s), yy, 1 - zz))
    sp2 = route(ends, lambda s, yy, zz: (end_of(s), yy + (1 if zz == 1 else -1), 1 - zz))
    mats = matrices(weights[0])

    sems = pltpu.SemaphoreType.DMA((20,))

    swp_b, near, sp1, sp2, mats = lax.optimization_barrier((swp_b, near, sp1, sp2, mats))

    def onward(value):
        return route(value, lambda s, yy, zz: (s, yy + 1 - 2 * zz, zz))

    far_b = onward(swp_b)
    bm, bd, dw = call(
        tick1_back,
        [shaped(16), shaped(4), ((2, 9 * C, 3 * C), F32)],
        [planes(8), planes(6), planes(8), planes(6), planes(6), planes(4), planes(6), planes(4), planes(8), planes(6), sems],
        (flags1, mats, nat_b, swp_b, near, far_b),
        2_000_000_000,
        [SMEM, VMEM] + [HBM] * 4,
        [HBM, HBM, VMEM],
    )

    def fwd_diag(s, yy, zz):
        r = fwd_side(s, zz)
        return (s + 1, yy + 1 - 2 * r, r)

    def back_diag(s, yy, zz):
        r = back_side(s, zz)
        return (s - 1, yy + 1 - 2 * r, r)

    bm2 = route(bm, lambda s, yy, zz: (s - 1, yy, back_side(s, zz)))
    bd2 = route(bd, back_diag)
    swp_f, bm = lax.optimization_barrier((swp_f, bm))
    far_f = onward(swp_f)
    fm, fd, ld, y1w = call(
        tick1_forward,
        [shaped(8), shaped(2), shaped(2), shaped(10)],
        [planes(8), planes(6), planes(6), planes(4), planes(8), planes(6), sems],
        (flags1, mats, nat_f, swp_f, near, far_f, last_own),
        1_000_000_000,
        [SMEM, VMEM] + [HBM] * 5,
        [HBM] * 4,
    )
    ld2 = route(ld, lambda s, yy, zz: (s if s == count - 1 else -1, yy + 1 - 2 * zz, zz))
    fd2 = route(fd, fwd_diag)
    fm2 = route(fm, lambda s, yy, zz: (s + 1, yy, fwd_side(s, zz)))

    bm2, bd2, fm2, fd2, ld2 = lax.optimization_barrier((bm2, bd2, fm2, fd2, ld2))
    out_b, parts = call(
        functools.partial(tick2_back, scale),
        [((4, 2 * R, W), BF16), ((slabs, slab_rows(slabs), W), BF16)],
        [planes(6), planes(4), planes(6), planes(4), planes(4), planes(2), planes(4), planes(2), planes(6), planes(4), sems],
        (flags2, mats, bm2, bd2, sp1, sp2, y1w, fm, ld2, dw),
        1_500_000_000,
        [SMEM, VMEM] + [HBM] * 7 + [VMEM],
        [VMEM, VMEM],
    )
    back = route(out_b, lambda s, yy, zz: (s - 1, yy, zz))
    parts = lax.all_to_all(parts, "slab", 0, 0, tiled=True)

    fm2, out_b = lax.optimization_barrier((fm2, out_b))
    (out_f,) = call(
        tick2_forward,
        [((2, 2 * R, W), BF16)],
        [planes(6), planes(4), planes(4), planes(2), planes(6), planes(4), sems],
        (flags2, mats, fm2, fd2, sp1, sp2, first_own),
        700_000_000,
        [SMEM, VMEM] + [HBM] * 5,
        [VMEM],
    )

    total = jnp.sum(wide(parts), axis=0)[: 2 * 9 * (C // slabs), : 3 * C]
    total = total.reshape(2, 9, C // slabs, 3, C).transpose(0, 4, 2, 1, 3).reshape(1, 2, C, -1)

    acts = jnp.where(is_last, out_f, back[:2])
    grads = jnp.where(is_last, flat_rows(loss_grad[1]), back[2:])
    return (*(v.reshape(fwd_in.shape) for v in (out_f, acts, grads)), total)


def solution(mesh):
    placed = (
        P("segment", None, None, "slab", None, None),
        P("segment", None, None, "slab", None, None),
        P("segment", None, None, "slab", None, None),
        P(None, None, "slab", None, None),
        P(None, None, None, "slab", None, None),
        P("segment", None, None, None),
    )
    return jax.shard_map(
        local,
        mesh=mesh,
        in_specs=placed,
        out_specs=(
            P("segment", None, None, "slab", None, None),
            P("segment", None, None, "slab", None, None),
            P("segment", None, None, "slab", None, None),
            P("segment", None, None, "slab"),
        ),
        check_vma=False,
    )
```

```python
import functools

import jax
import jax.numpy as jnp
from jax import lax
from jax.experimental import pallas as pl
from jax.experimental.pallas import tpu as pltpu
from jax.sharding import PartitionSpec as P

F32 = jnp.float32
BF16 = jnp.bfloat16
C = 32
H = 4
R = C * H
W = 128
SNAKE = 16


def wide(v):
    return v.astype(F32)


def silu(v):
    v = wide(v)
    return (v / (1.0 + jnp.exp(-v))).astype(BF16)


def slope(v):
    v = wide(v)
    sig = 1.0 / (1.0 + jnp.exp(-v))
    return sig * (1.0 + v * (1.0 - sig))


def conv_planes(w_ref, field, start, count, use):
    lane = lax.broadcasted_iota(jnp.int32, (R, W), 1)
    for d in range(0, count, 2):
        n = min(2, count - d)
        x = jnp.concatenate(
            [jnp.concatenate([field[start + d + k + a] for a in range(3)], axis=0) for k in range(n)], axis=1
        )
        y = jnp.dot(w_ref[...], x, preferred_element_type=F32)
        for k in range(n):
            cols = slice(k * W, (k + 1) * W)
            left = jnp.where(lane >= 1, pltpu.roll(y[:R, cols], 1, 1), 0.0)
            right = jnp.where(lane < W - 1, pltpu.roll(y[2 * R :, cols], W - 1, 1), 0.0)
            use(start + d + k, y[R : 2 * R, cols] + left + right)


def mask(d, v, inner, keep):
    if d == 0:
        v = v * keep[0]
    if d == inner - 1:
        v = v * keep[1]
    return v


def forward(n, keep, w_ref, fb, fa, out_a, out_b, act_b, act_a):
    inner = n - 2
    for p in range(n):
        act_b[p] = silu(fb[p])

    def one(d, v):
        out = mask(d, wide(fa[d]) + v, inner, keep).astype(BF16)
        out_a[d] = out
        act_a[d] = silu(out)

    conv_planes(w_ref.at[0], act_b, 0, inner, one)

    def two(d, v):
        out_b[d] = (wide(fb[d + 2]) + v).astype(BF16)

    conv_planes(w_ref.at[1], act_a, 0, inner - 2, two)


def backward(keep, w_ref, bb, ba, db, da, rec_a, rec_b, grad_a, grad_b, act_b, act_a, first, count):
    n, inner = (8, 6)
    for p in range(n):
        act_b[p] = silu(bb[p])

    def one(d, v):
        out = mask(d, wide(ba[d]) - v, inner, keep).astype(BF16)
        rec_a[d] = out
        act_a[d] = silu(out)

    conv_planes(w_ref.at[1], act_b, 0, inner, one)

    def two(d, v):
        grad_a[d] = mask(d, wide(da[d]) + slope(bb[d + 1]) * v, inner, keep).astype(BF16)

    conv_planes(w_ref.at[3], db, 0, inner, two)

    def three(d, v):
        rec_b[d] = (wide(bb[d + 2]) - v).astype(BF16)

    conv_planes(w_ref.at[0], act_a, first, count, three)

    def four(d, v):
        grad_b[d] = (wide(db[d + 2]) + slope(rec_a[d + 1]) * v).astype(BF16)

    conv_planes(w_ref.at[2], grad_a, first, count, four)


class Copies:
    def __init__(self, sems):
        self.sems, self.groups, self.n = (sems, [], 0)

    def add(self, pairs, when=None):
        pairs = list(pairs)
        made = [pltpu.make_async_copy(src, dst, self.sems.at[self.n + k]) for k, (src, dst) in enumerate(pairs)]
        self.n += len(made)
        self.groups.append((when, made))

    def each(self, what):
        for when, made in self.groups:
            def run(made=made):
                for copy in made:
                    getattr(copy, what)()

            if when is None:
                run()
            else:
                pl.when(when)(run)

    def start(self):
        self.each("start")

    def wait(self):
        self.each("wait")

    def run(self):
        self.start()
        self.wait()


def at(ref, first, count):
    return ref.at[pl.ds(first, count)]


def window1(zh, b, a, nat_b, nat_a, swp_b, swp_a, near_b, near_a, far_b, far_a):
    return [
        (nat_b, at(b, 2 + 2 * zh, 2)),
        (swp_b, at(b, 4 - 2 * zh, 2)),
        (near_b, at(b, 6 - 6 * zh, 2)),
        (far_b, at(b, 6 * zh, 2)),
        (nat_a, at(a, 1 + 2 * zh, 2)),
        (swp_a, at(a, 3 - 2 * zh, 2)),
        (near_a, at(a, 5 - 5 * zh, 1)),
        (far_a, at(a, 5 * zh, 1)),
    ]


def special(zh, b, a, own, sp1, sp2):
    return [
        (own[1], at(b, 2, 2)),
        (sp1.at[1], at(b, 4 - 4 * zh, 2)),
        (sp2.at[1], at(b, 4 * zh, 2)),
        (own[0], at(a, 1, 2)),
        (at(sp1.at[0], zh, 1), at(a, 3 - 3 * zh, 1)),
        (at(sp2.at[0], 1 - zh, 1), at(a, 3 * zh, 1)),
    ]


def keeps(flags):
    return (flags[1].astype(F32), flags[2].astype(F32))


def weight_sums(db, grad_a, act_b, act_a):
    return (
        wgrad_pair(at(grad_a, 1, 4), act_a),
        wgrad_pair(at(db, 2, 4), at(act_b, 1, 6)),
    )


def tick1_back(flags, w_ref, nat, swp, near, far, bm, bl, bh, dw, *scratch):
    bb, ba, db, da, rec_a, rec_b, grad_a, grad_b, act_b, act_a, sems = scratch
    zh = flags[0]
    load = Copies(sems)
    for k, (b, a) in enumerate(((bb, ba), (db, da))):
        load.add(
            window1(
                zh, b, a, at(nat, 2 * k, 2), at(nat, 4 + 2 * k, 2), at(swp, 2 * k, 2), at(swp, 4 + 2 * k, 2),
                at(near, 2 * k, 2), at(near, 4 + 2 * k + zh, 1), at(far, 2 * k, 2), at(far, 5 + 2 * k - zh, 1),
            )
        )
    load.run()
    backward(keeps(flags), w_ref, bb, ba, db, da, rec_a, rec_b, grad_a, grad_b, act_b, act_a, 0, 4)
    save = Copies(sems)
    save.add([
        (rec_b, at(bm, 0, 4)),
        (grad_b, at(bm, 4, 4)),
        (rec_a, at(bm, 8, 6)),
        (grad_a, at(bm, 14, 6)),
        (at(rec_b, 2, 2), at(bl, 0, 2)),
        (at(grad_b, 2, 2), at(bl, 2, 2)),
        (at(rec_b, 0, 2), at(bh, 0, 2)),
        (at(grad_b, 0, 2), at(bh, 2, 2)),
    ])
    save.start()
    dw[0], dw[1] = weight_sums(db, grad_a, act_b, act_a)
    save.wait()


def tick1_forward(flags, w_ref, nat, swp, near, far, last_own, fm, fd, ll, lh, y1w, *scratch):
    fb, fa, out_a, out_b, act_b, act_a, sems = scratch
    zh, fz = (flags[0], flags[3])
    load = Copies(sems)
    load.add(
        window1(
            zh, fb, fa, at(nat.at[0], 0, 2), at(nat.at[0], 2, 2), at(swp, 0, 2), at(swp, 2, 2),
            at(near, 8, 2), at(near, 10 + zh, 1), at(far, 0, 2), at(far, 3 - zh, 1),
        )
    )
    load.run()
    forward(8, keeps(flags), w_ref, fb, fa, out_a, out_b, act_b, act_a)
    save = Copies(sems)
    save.add([
        (out_b, at(fm, 0, 4)),
        (at(out_a, 2 * fz, 4), at(fm, 4, 4)),
        (at(out_b, 2 - 2 * fz, 2), fd),
        (at(out_a, 3, 1), at(ll, 0, 1)),
        (at(out_b, 3, 1), at(ll, 1, 1)),
        (at(out_a, 2, 1), at(lh, 0, 1)),
        (at(out_b, 0, 1), at(lh, 1, 1)),
        (out_a, at(y1w, 0, 6)),
        (last_own.at[0], at(y1w, 6, 2)),
        (last_own.at[1], at(y1w, 8, 2)),
    ])
    save.run()


def tick2_back(
    scale, flags, w_ref, bm, bl, bh, sp1, sp2, sp3, y1w, own, ll, lh, dw, out, parts, *scratch
):
    bb, ba, db, da, rec_a, rec_b, grad_a, grad_b, act_b, act_a, sems = scratch
    zh = flags[0]
    load = Copies(sems)
    load.add(
        window1(
            zh, db, da, at(y1w, 8, 2), at(y1w, 6, 2), sp1.at[1], sp1.at[0],
            sp3.at[1], at(sp3.at[0], zh, 1), sp2.at[1], at(sp2.at[0], 1 - zh, 1),
        )
        + [
            (at(y1w, 0, 6), at(bb, 1, 6)),
            (at(ll, 0, 1), at(bb, 0, 1)),
            (at(lh, 0, 1), at(bb, 7, 1)),
            (at(own, 0, 4), at(ba, 1, 4)),
            (at(ll, 1, 1), at(ba, 0, 1)),
            (at(lh, 1, 1), at(ba, 5, 1)),
        ],
        flags[6] == 1,
    )
    load.add(
        [
            (at(bl, 0, 2), at(bb, 0, 2)),
            (at(bm, 0, 4), at(bb, 2, 4)),
            (at(bh, 0, 2), at(bb, 6, 2)),
            (at(bl, 2, 2), at(db, 0, 2)),
            (at(bm, 4, 4), at(db, 2, 4)),
            (at(bh, 2, 2), at(db, 6, 2)),
            (at(bm, 8, 6), ba),
            (at(bm, 14, 6), da),
        ],
        flags[6] == 0,
    )
    load.start()
    order, back_order = (slab_order(2 * parts.shape[0], zh), to_outside())
    load.wait()
    backward(keeps(flags), w_ref, bb, ba, db, da, rec_a, rec_b, grad_a, grad_b, act_b, act_a, 2 * zh, 2)
    own_a, own_b = (pl.ds(1 + 2 * zh, 2), pl.ds(2 * zh, 2))
    pieces = [rec_b[own_b], rec_a[own_a], grad_a[own_a], grad_b[own_b]]
    for k, v in enumerate(reorder(back_order, [p.reshape(2 * R, W) for p in pieces])):
        out[k] = v
    sums = [dw[k] + v for k, v in enumerate(weight_sums(db, grad_a, act_b, act_a))]
    sums = jnp.concatenate([(v * scale).astype(BF16) for v in sums], axis=0)
    ordered = jnp.dot(order, sums, preferred_element_type=F32).astype(BF16)
    parts[:, :, : 3 * C] = ordered.reshape(*parts.shape[:2], 3 * C)
    parts[:, :, 3 * C :] = jnp.zeros((*parts.shape[:2], W - 3 * C), BF16)


def tick2_forward(flags, w_ref, fm, fd, sp1, sp2, first_own, out, *scratch):
    fb, fa, out_a, out_b, act_b, act_a, sems = scratch
    zh, first = (flags[0], flags[3])
    main, halo = (2 - 2 * zh, 4 * zh)
    load = Copies(sems)
    load.add(special(zh, fb, fa, (first_own.at[0], first_own.at[1]), sp1, sp2), first == 1)
    load.add(
        [(at(fm, 0, 4), at(fb, main, 4)), (fd, at(fb, halo, 2)), (at(fm, 4, 4), fa)],
        first == 0,
    )
    load.run()
    forward(6, keeps(flags), w_ref, fb, fa, out_a, out_b, act_b, act_a)
    for k, v in enumerate(reorder(to_outside(), [p.reshape(2 * R, W) for p in (out_a[1:3], out_b[...])])):
        out[k] = v


def wgrad_pair(g_ref, u_ref):
    lane = lax.broadcasted_iota(jnp.int32, (C, W), 1)
    zero = jnp.zeros((C, W), BF16)
    left, right = ([], [])
    for d in range(g_ref.shape[0]):
        for h in range(H):
            g = wide(g_ref[d, h * C : (h + 1) * C])
            down = jnp.where(lane < W - 1, pltpu.roll(g, W - 1, 1), 0.0)
            up = jnp.where(lane >= 1, pltpu.roll(g, 1, 1), 0.0)
            left.append(jnp.concatenate([down, g, up], axis=0).astype(BF16))
            rows = []
            for a in range(3):
                for b in range(3):
                    at = h + b - 1
                    rows.append(u_ref[d + a, at * C : (at + 1) * C] if 0 <= at < H else zero)
            right.append(jnp.concatenate(rows, axis=0))
    return lax.dot_general(
        jnp.concatenate(right, axis=1),
        jnp.concatenate(left, axis=1),
        (((1,), (1,)), ((), ())),
        preferred_element_type=F32,
    )


def bands_kernel(rows, out):
    lane = lax.broadcasted_iota(jnp.int32, (C, R), 1)
    for kind in range(4):
        for c in range(3):
            for a in range(3):
                tile = wide(rows[kind, c, :, a * R : (a + 1) * R])
                for h in range(H):
                    moved = tile if h == 1 else pltpu.roll(tile, ((h - 1) * C) % R, 1)
                    if h == 0:
                        moved = jnp.where(lane < 2 * C, moved, 0.0)
                    if h == 3:
                        moved = jnp.where(lane >= 2 * C, moved, 0.0)
                    at_row = (c * H + h) * C
                    out[kind, at_row : at_row + C, a * R : (a + 1) * R] = moved.astype(BF16)


VMEM = pl.BlockSpec(memory_space=pltpu.VMEM)
SMEM = pl.BlockSpec(memory_space=pltpu.SMEM)
HBM = pl.BlockSpec(memory_space=pltpu.HBM)


def call(kernel, outs, scratch, args, flops, specs, out_specs, mib=16):
    return pl.pallas_call(
        kernel,
        out_shape=tuple(jax.ShapeDtypeStruct(s, t) for s, t in outs),
        in_specs=specs,
        out_specs=tuple(out_specs),
        scratch_shapes=scratch,
        compiler_params=pltpu.CompilerParams(vmem_limit_bytes=mib * 2**20),
        cost_estimate=pl.CostEstimate(flops=flops, bytes_accessed=4_000_000, transcendentals=400_000),
    )(*args)


def slab_rows(slabs):
    return -(-2 * 9 * C // (16 * slabs)) * 16


def slab_order(slabs, zh):
    per = C // slabs
    low, rows = (per.bit_length() - 1, slab_rows(slabs))

    def target(n):
        slab = (n & (C - 1)) >> low
        row = (slab >> 1) * rows + (n >> 5) * per + (n & (per - 1))
        return jnp.where((slab & 1) == zh, row, -1)

    return one_hot(slabs // 2 * rows, 2 * 9 * C, target)


def planes(*lead):
    return pltpu.VMEM((*lead, R, W), BF16)


def shaped(*lead):
    return ((*lead, R, W), BF16)


def flat_rows(value):
    return value.reshape(value.shape[0], -1, W)


def one_hot(rows, cols, target):
    row = lax.broadcasted_iota(jnp.int32, (rows, cols), 0)
    col = lax.broadcasted_iota(jnp.int32, (rows, cols), 1)
    return jnp.where(row == target(col), 1.0, 0.0).astype(BF16)


def to_inside():
    return one_hot(2 * R, 2 * R, lambda n: (n & 7) * C + (n >> 3))


def to_outside():
    return one_hot(2 * R, 2 * R, lambda n: (n & (C - 1)) * 8 + (n >> 5))


def reorder(matrix, pieces):
    both = jnp.dot(matrix, jnp.concatenate(pieces, axis=1), preferred_element_type=F32).astype(BF16)
    return [both[:, k * W : (k + 1) * W] for k in range(len(pieces))]


def prepare_kernel(fwd_hbm, acts_hbm, grads_hbm, nat_b, nat_f, near, fwd, acts, grads, sems):
    load = Copies(sems)
    load.add([(fwd_hbm, fwd), (acts_hbm, acts), (grads_hbm, grads)])
    load.start()
    order = to_inside()
    load.wait()
    streams = reorder(order, [acts[0], grads[1], acts[1], grads[0], fwd[1], fwd[0]])
    for k, v in enumerate(streams):
        for half, plane in enumerate((v[:R], v[R:])):
            near[2 * k + half] = plane
            if k < 4:
                nat_b[2 * k + half] = plane
            else:
                for copy in range(2):
                    nat_f[copy, 2 * (k - 4) + half] = plane


def prepare_ends_kernel(flags, batch, loss, first_own, last_own, ends):
    x1, x2, d1, d2 = reorder(to_inside(), [batch[0], batch[1], loss[0], loss[1]])
    for ref, pair in ((first_own, (x1, x2)), (last_own, (d1, d2))):
        for k in range(2):
            ref[k, 0] = pair[k][:R]
            ref[k, 1] = pair[k][R:]
    first = flags[5] == 1

    @pl.when(first)
    def _():
        ends[...] = first_own[...]

    @pl.when(jnp.logical_not(first))
    def _():
        ends[...] = last_own[...]


def matrices(flat):
    k = flat.reshape(2, C, C, 3, 3, 3)
    turned = jnp.flip(k, (3, 4, 5)).transpose(0, 2, 1, 3, 4, 5)
    both = jnp.concatenate([k, turned])
    rows = both.transpose(0, 5, 1, 3, 4, 2)
    rows = jnp.pad(rows, ((0, 0), (0, 0), (0, 0), (0, 0), (0, 1), (0, 0))).reshape(4, 3, C, 3 * R)
    (out,) = call(bands_kernel, [((4, 3 * R, 3 * R), BF16)], [], (rows,), 1_000_000, [VMEM], [VMEM])
    return out


def local(fwd_in, back_out, back_grad, batch_next, loss_grad, weights):
    seg = lax.axis_index("segment")
    slab = lax.axis_index("slab")
    count = lax.axis_size("segment")
    slabs = lax.axis_size("slab")
    ny = slabs // 2
    y, zh = (slab // 2, slab % 2)
    scale = float(fwd_in.shape[3] * slabs * fwd_in.shape[4] * fwd_in.shape[5]) ** (-0.5)

    def route(value, to):
        pairs = []
        for s in range(count):
            for yy in range(ny):
                for zz in range(2):
                    target = to(s, yy, zz)
                    if target is None:
                        continue
                    ts, ty, tz = target
                    if 0 <= ts < count and 0 <= ty < ny:
                        pairs.append((s * slabs + 2 * yy + zz, ts * slabs + 2 * ty + tz))
        return lax.ppermute(value, ("segment", "slab"), pairs)

    def fwd_side(s, zz):
        return 1 - zz if s % SNAKE == SNAKE - 1 and s < count - 1 else zz

    def back_side(s, zz):
        return 1 - zz if s % SNAKE == 0 and s > 0 else zz

    fz = jnp.where((seg % SNAKE == SNAKE - 1) & (seg < count - 1), 1 - zh, zh)
    is_first, is_last = (seg == 0, seg == count - 1)

    def swap(value):
        return route(value, lambda s, yy, zz: (s, yy, 1 - zz))

    def as_flags(*values):
        return jnp.stack([jnp.asarray(v).astype(jnp.int32) for v in values])

    from_first, from_last = (14 % count, (count - 15) % count)
    flags1 = as_flags(zh, y > 0, y < ny - 1, fz, 0, seg == from_first, is_last)
    flags2 = as_flags(zh, (y > 0) | (zh == 1), (y < ny - 1) | (zh == 0), is_first, is_last)
    nat_b, nat_f, near = call(
        prepare_kernel,
        [shaped(8), shaped(2, 4), shaped(12)],
        [pltpu.VMEM((2, 2 * R, W), BF16)] * 3 + [pltpu.SemaphoreType.DMA((3,))],
        (flat_rows(fwd_in[0]), flat_rows(back_out[0]), flat_rows(back_grad[0])),
        100_000_000,
        [HBM] * 3,
        [VMEM] * 3,
        58,
    )
    swp_b = swap(nat_b)
    pairs = [[2 * k, 2 * k + 1] for k in range(ny)]
    all_f = lax.all_to_all(nat_f, "slab", 0, 0, axis_index_groups=pairs, tiled=True)
    near = route(near, lambda s, yy, zz: (s, yy - 1 + 2 * zz, zz))
    first_own, last_own, ends = call(
        prepare_ends_kernel,
        [shaped(2, 2)] * 3,
        [],
        (flags1, flat_rows(batch_next), flat_rows(loss_grad[0])),
        100_000_000,
        [SMEM] + [VMEM] * 2,
        [VMEM] * 3,
    )

    def end_of(s):
        return 0 if s == from_first else count - 1 if s == from_last else -1

    sp1 = route(ends, lambda s, yy, zz: (end_of(s), yy, 1 - zz))
    sp2 = route(ends, lambda s, yy, zz: (end_of(s), yy + (1 if zz == 1 else -1), 1 - zz))
    sp3 = route(last_own, lambda s, yy, zz: (count - 1 if s == count - 2 else -1, yy - 1 + 2 * zz, zz))
    mats = matrices(weights[0])

    sems = pltpu.SemaphoreType.DMA((24,))

    swp_b, near, sp1, sp2, sp3, mats = lax.optimization_barrier((swp_b, near, sp1, sp2, sp3, mats))

    def onward(value):
        return route(value, lambda s, yy, zz: (s, yy + 1 - 2 * zz, zz))

    far_b = onward(swp_b)
    bm, bl, bh, dw = call(
        tick1_back,
        [shaped(20), shaped(4), shaped(4), ((2, 9 * C, 3 * C), F32)],
        [planes(8), planes(6), planes(8), planes(6), planes(6), planes(4), planes(6), planes(4), planes(8), planes(6), sems],
        (flags1, mats, nat_b, swp_b, near, far_b),
        2_000_000_000,
        [SMEM, VMEM] + [HBM] * 4,
        [HBM, HBM, HBM, VMEM],
    )

    def fwd_diag(s, yy, zz):
        r = fwd_side(s, zz)
        return (s + 1, yy + 1 - 2 * r, r)

    bm2 = route(bm, lambda s, yy, zz: (s - 1, yy, back_side(s, zz)))
    bl2 = route(bl, lambda s, yy, zz: (s - 1, yy + 1, back_side(s, zz)))
    bh2 = route(bh, lambda s, yy, zz: (s - 1, yy - 1, back_side(s, zz)))

    all_f, bm = lax.optimization_barrier((all_f, bm))
    swp_f = jnp.where(zh == 0, all_f[1], all_f[0])
    far_f = onward(swp_f)
    far_f, bl2, bh2 = lax.optimization_barrier((far_f, bl2, bh2))
    fm, fd, ll, lh, y1w = call(
        tick1_forward,
        [shaped(8), shaped(2), shaped(2), shaped(2), shaped(10)],
        [planes(8), planes(6), planes(6), planes(4), planes(8), planes(6), sems],
        (flags1, mats, nat_f, swp_f, near, far_f, last_own),
        1_000_000_000,
        [SMEM, VMEM] + [HBM] * 5,
        [HBM] * 5,
    )
    ll2 = route(ll, lambda s, yy, zz: (s if s == count - 1 else -1, yy + 1, zz))
    lh2 = route(lh, lambda s, yy, zz: (s if s == count - 1 else -1, yy - 1, zz))
    fd2 = route(fd, fwd_diag)
    fm2 = route(fm, lambda s, yy, zz: (s + 1, yy, fwd_side(s, zz)))

    bm2, bl2, bh2, fm2, fd2, ll2, lh2 = lax.optimization_barrier((bm2, bl2, bh2, fm2, fd2, ll2, lh2))
    out_b, parts = call(
        functools.partial(tick2_back, scale),
        [((4, 2 * R, W), BF16), ((ny, slab_rows(slabs), W), BF16)],
        [planes(8), planes(6), planes(8), planes(6), planes(6), planes(4), planes(6), planes(4), planes(8), planes(6), sems],
        (flags1, mats, bm2, bl2, bh2, sp1, sp2, sp3, y1w, fm, ll2, lh2, dw),
        1_500_000_000,
        [SMEM, VMEM] + [HBM] * 10 + [VMEM],
        [VMEM, VMEM],
    )
    back = route(out_b, lambda s, yy, zz: (s - 1, yy, zz))
    columns = [[2 * k + j for k in range(ny)] for j in range(2)]
    parts = lax.all_to_all(parts, "slab", 0, 0, axis_index_groups=columns, tiled=True)

    fm2, out_b = lax.optimization_barrier((fm2, out_b))
    (out_f,) = call(
        tick2_forward,
        [((2, 2 * R, W), BF16)],
        [planes(6), planes(4), planes(4), planes(2), planes(6), planes(4), sems],
        (flags2, mats, fm2, fd2, sp1, sp2, first_own),
        700_000_000,
        [SMEM, VMEM] + [HBM] * 5,
        [VMEM],
    )

    total = jnp.sum(wide(parts), axis=0)[: 2 * 9 * (C // slabs), : 3 * C]
    total = total.reshape(2, 9, C // slabs, 3, C).transpose(0, 4, 2, 1, 3).reshape(1, 2, C, -1)

    acts = jnp.where(is_last, out_f, back[:2])
    grads = jnp.where(is_last, flat_rows(loss_grad[1]), back[2:])
    return (*(v.reshape(fwd_in.shape) for v in (out_f, acts, grads)), total)


def solution(mesh):
    placed = (
        P("segment", None, None, "slab", None, None),
        P("segment", None, None, "slab", None, None),
        P("segment", None, None, "slab", None, None),
        P(None, None, "slab", None, None),
        P(None, None, None, "slab", None, None),
        P("segment", None, None, None),
    )
    return jax.shard_map(
        local,
        mesh=mesh,
        in_specs=placed,
        out_specs=(
            P("segment", None, None, "slab", None, None),
            P("segment", None, None, "slab", None, None),
            P("segment", None, None, "slab", None, None),
            P("segment", None, None, "slab"),
        ),
        check_vma=False,
    )
```

```python
import functools

import jax
import jax.numpy as jnp
from jax import lax
from jax.experimental import pallas as pl
from jax.experimental.pallas import tpu as pltpu
from jax.sharding import PartitionSpec as P

F32 = jnp.float32
BF16 = jnp.bfloat16
C = 32
H = 4
R = C * H
W = 128
SNAKE = 16


def wide(v):
    return v.astype(F32)


def silu(v):
    v = wide(v)
    return (v / (1.0 + jnp.exp(-v))).astype(BF16)


def slope(v):
    v = wide(v)
    sig = 1.0 / (1.0 + jnp.exp(-v))
    return sig * (1.0 + v * (1.0 - sig))


def conv_planes(w_ref, field, start, count, use):
    lane = lax.broadcasted_iota(jnp.int32, (R, W), 1)
    for d in range(0, count, 2):
        n = min(2, count - d)
        x = jnp.concatenate(
            [jnp.concatenate([field[start + d + k + a] for a in range(3)], axis=0) for k in range(n)], axis=1
        )
        y = jnp.dot(w_ref[...], x, preferred_element_type=F32)
        for k in range(n):
            cols = slice(k * W, (k + 1) * W)
            left = jnp.where(lane >= 1, pltpu.roll(y[:R, cols], 1, 1), 0.0)
            right = jnp.where(lane < W - 1, pltpu.roll(y[2 * R :, cols], W - 1, 1), 0.0)
            use(start + d + k, y[R : 2 * R, cols] + left + right)


def mask(d, v, inner, keep):
    if d == 0:
        v = v * keep[0]
    if d == inner - 1:
        v = v * keep[1]
    return v


def forward(n, keep, w_ref, fb, fa, out_a, out_b, act_b, act_a):
    inner = n - 2
    for p in range(n):
        act_b[p] = silu(fb[p])

    def one(d, v):
        out = mask(d, wide(fa[d]) + v, inner, keep).astype(BF16)
        out_a[d] = out
        act_a[d] = silu(out)

    conv_planes(w_ref.at[0], act_b, 0, inner, one)

    def two(d, v):
        out_b[d] = (wide(fb[d + 2]) + v).astype(BF16)

    conv_planes(w_ref.at[1], act_a, 0, inner - 2, two)


def backward(keep, w_ref, bb, ba, db, da, rec_a, rec_b, grad_a, grad_b, act_b, act_a, first, count):
    n, inner = (8, 6)
    for p in range(n):
        act_b[p] = silu(bb[p])

    def one(d, v):
        out = mask(d, wide(ba[d]) - v, inner, keep).astype(BF16)
        rec_a[d] = out
        act_a[d] = silu(out)

    conv_planes(w_ref.at[1], act_b, 0, inner, one)

    def two(d, v):
        grad_a[d] = mask(d, wide(da[d]) + slope(bb[d + 1]) * v, inner, keep).astype(BF16)

    conv_planes(w_ref.at[3], db, 0, inner, two)

    def three(d, v):
        rec_b[d] = (wide(bb[d + 2]) - v).astype(BF16)

    conv_planes(w_ref.at[0], act_a, first, count, three)

    def four(d, v):
        grad_b[d] = (wide(db[d + 2]) + slope(rec_a[d + 1]) * v).astype(BF16)

    conv_planes(w_ref.at[2], grad_a, first, count, four)


def move(pairs):
    for src, dst in pairs:
        for k in range(dst.shape[0]):
            dst[k] = src[k]


def at(ref, first, count):
    return ref.at[pl.ds(first, count)]


def window1(zh, b, a, nat_b, nat_a, swp_b, swp_a, near_b, near_a, far_b, far_a):
    return [
        (nat_b, at(b, 2 + 2 * zh, 2)),
        (swp_b, at(b, 4 - 2 * zh, 2)),
        (near_b, at(b, 6 - 6 * zh, 2)),
        (far_b, at(b, 6 * zh, 2)),
        (nat_a, at(a, 1 + 2 * zh, 2)),
        (swp_a, at(a, 3 - 2 * zh, 2)),
        (near_a, at(a, 5 - 5 * zh, 1)),
        (far_a, at(a, 5 * zh, 1)),
    ]


def special(zh, b, a, own, sp1, sp2):
    return [
        (own[1], at(b, 2, 2)),
        (sp1.at[1], at(b, 4 - 4 * zh, 2)),
        (sp2.at[1], at(b, 4 * zh, 2)),
        (own[0], at(a, 1, 2)),
        (at(sp1.at[0], zh, 1), at(a, 3 - 3 * zh, 1)),
        (at(sp2.at[0], 1 - zh, 1), at(a, 3 * zh, 1)),
    ]


def keeps(flags):
    return (flags[1].astype(F32), flags[2].astype(F32))


def weight_sums(db, grad_a, act_b, act_a):
    return (
        wgrad_pair(at(grad_a, 1, 4), act_a),
        wgrad_pair(at(db, 2, 4), at(act_b, 1, 6)),
    )


def tick1_window(zh, b, a, b_at, a_at, nat, swp, near, far):
    move(
        window1(
            zh, b, a, at(nat, b_at, 2), at(nat, a_at, 2), at(swp, b_at, 2), at(swp, a_at, 2),
            at(near, b_at, 2), at(near, a_at + zh, 1), at(far, b_at, 2), at(far, a_at + 1 - zh, 1),
        )
    )


def tick1_back(flags, w_ref, nat, swp, near, far, bm, bl, bh, dw, *scratch):
    bb, ba, db, da, rec_a, rec_b, grad_a, grad_b, act_b, act_a = scratch
    for k, (b, a) in enumerate(((bb, ba), (db, da))):
        tick1_window(flags[0], b, a, 2 * k, 4 + 2 * k, nat, swp, near, far)
    backward(keeps(flags), w_ref, bb, ba, db, da, rec_a, rec_b, grad_a, grad_b, act_b, act_a, 0, 4)
    move([
        (rec_b, at(bm, 0, 4)),
        (grad_b, at(bm, 4, 4)),
        (rec_a, at(bm, 8, 6)),
        (grad_a, at(bm, 14, 6)),
        (at(rec_b, 2, 2), at(bl, 0, 2)),
        (at(grad_b, 2, 2), at(bl, 2, 2)),
        (at(rec_b, 0, 2), at(bh, 0, 2)),
        (at(grad_b, 0, 2), at(bh, 2, 2)),
    ])
    dw[0], dw[1] = weight_sums(db, grad_a, act_b, act_a)


def tick1_forward(flags, w_ref, nat, swp, near, far, last_own, fm, fd, ll, lh, y1w, *scratch):
    fb, fa, out_a, out_b, act_b, act_a = scratch
    fz = flags[3]
    tick1_window(flags[0], fb, fa, 8, 10, nat, swp, near, far)
    forward(8, keeps(flags), w_ref, fb, fa, out_a, out_b, act_b, act_a)
    move([
        (out_b, at(fm, 0, 4)),
        (at(out_a, 2 * fz, 4), at(fm, 4, 4)),
        (at(out_b, 2 - 2 * fz, 2), fd),
        (at(out_a, 3, 1), at(ll, 0, 1)),
        (at(out_b, 3, 1), at(ll, 1, 1)),
        (at(out_a, 2, 1), at(lh, 0, 1)),
        (at(out_b, 0, 1), at(lh, 1, 1)),
        (out_a, at(y1w, 0, 6)),
        (last_own.at[0], at(y1w, 6, 2)),
        (last_own.at[1], at(y1w, 8, 2)),
    ])


def tick2_back(
    scale, flags, w_ref, bm, bl, bh, sp1, sp2, sp3, y1w, own, ll, lh, dw, out, parts, *scratch
):
    bb, ba, db, da, rec_a, rec_b, grad_a, grad_b, act_b, act_a = scratch
    zh = flags[0]

    @pl.when(flags[6] == 1)
    def _():
        move(window1(
            zh, db, da, at(y1w, 8, 2), at(y1w, 6, 2), sp1.at[1], sp1.at[0],
            sp3.at[1], at(sp3.at[0], zh, 1), sp2.at[1], at(sp2.at[0], 1 - zh, 1),
        ))
        move([
            (at(y1w, 0, 6), at(bb, 1, 6)),
            (at(ll, 0, 1), at(bb, 0, 1)),
            (at(lh, 0, 1), at(bb, 7, 1)),
            (at(own, 0, 4), at(ba, 1, 4)),
            (at(ll, 1, 1), at(ba, 0, 1)),
            (at(lh, 1, 1), at(ba, 5, 1)),
        ])

    @pl.when(flags[6] == 0)
    def _():
        move([
            (at(bl, 0, 2), at(bb, 0, 2)),
            (at(bm, 0, 4), at(bb, 2, 4)),
            (at(bh, 0, 2), at(bb, 6, 2)),
            (at(bl, 2, 2), at(db, 0, 2)),
            (at(bm, 4, 4), at(db, 2, 4)),
            (at(bh, 2, 2), at(db, 6, 2)),
            (at(bm, 8, 6), ba),
            (at(bm, 14, 6), da),
        ])

    order, back_order = (slab_order(2 * parts.shape[0], zh), to_outside())
    backward(keeps(flags), w_ref, bb, ba, db, da, rec_a, rec_b, grad_a, grad_b, act_b, act_a, 2 * zh, 2)
    own_a, own_b = (pl.ds(1 + 2 * zh, 2), pl.ds(2 * zh, 2))
    pieces = [rec_b[own_b], rec_a[own_a], grad_a[own_a], grad_b[own_b]]
    for k, v in enumerate(reorder(back_order, [p.reshape(2 * R, W) for p in pieces])):
        out[k] = v
    sums = [dw[k] + v for k, v in enumerate(weight_sums(db, grad_a, act_b, act_a))]
    sums = jnp.concatenate([(v * scale).astype(BF16) for v in sums], axis=0)
    ordered = jnp.dot(order, sums, preferred_element_type=F32).astype(BF16)
    parts[:, :, : 3 * C] = ordered.reshape(*parts.shape[:2], 3 * C)
    parts[:, :, 3 * C :] = jnp.zeros((*parts.shape[:2], W - 3 * C), BF16)


def tick2_forward(flags, w_ref, fm, fd, sp1, sp2, first_own, out, *scratch):
    fb, fa, out_a, out_b, act_b, act_a = scratch
    zh, first = (flags[0], flags[3])

    @pl.when(first == 1)
    def _():
        move(special(zh, fb, fa, (first_own.at[0], first_own.at[1]), sp1, sp2))

    @pl.when(first == 0)
    def _():
        move([(at(fm, 0, 4), at(fb, 2 - 2 * zh, 4)), (fd, at(fb, 4 * zh, 2)), (at(fm, 4, 4), fa)])

    forward(6, keeps(flags), w_ref, fb, fa, out_a, out_b, act_b, act_a)
    for k, v in enumerate(reorder(to_outside(), [p.reshape(2 * R, W) for p in (out_a[1:3], out_b[...])])):
        out[k] = v


def wgrad_pair(g_ref, u_ref):
    lane = lax.broadcasted_iota(jnp.int32, (C, W), 1)
    zero = jnp.zeros((C, W), BF16)
    left, right = ([], [])
    for d in range(g_ref.shape[0]):
        for h in range(H):
            g = wide(g_ref[d, h * C : (h + 1) * C])
            down = jnp.where(lane < W - 1, pltpu.roll(g, W - 1, 1), 0.0)
            up = jnp.where(lane >= 1, pltpu.roll(g, 1, 1), 0.0)
            left.append(jnp.concatenate([down, g, up], axis=0).astype(BF16))
            rows = []
            for a in range(3):
                for b in range(3):
                    at = h + b - 1
                    rows.append(u_ref[d + a, at * C : (at + 1) * C] if 0 <= at < H else zero)
            right.append(jnp.concatenate(rows, axis=0))
    return lax.dot_general(
        jnp.concatenate(right, axis=1),
        jnp.concatenate(left, axis=1),
        (((1,), (1,)), ((), ())),
        preferred_element_type=F32,
    )


def bands_kernel(rows, out):
    lane = lax.broadcasted_iota(jnp.int32, (C, R), 1)
    for kind in range(4):
        for c in range(3):
            for a in range(3):
                tile = wide(rows[kind, c, :, a * R : (a + 1) * R])
                for h in range(H):
                    moved = tile if h == 1 else pltpu.roll(tile, ((h - 1) * C) % R, 1)
                    if h == 0:
                        moved = jnp.where(lane < 2 * C, moved, 0.0)
                    if h == 3:
                        moved = jnp.where(lane >= 2 * C, moved, 0.0)
                    at_row = (c * H + h) * C
                    out[kind, at_row : at_row + C, a * R : (a + 1) * R] = moved.astype(BF16)


VMEM = pl.BlockSpec(memory_space=pltpu.VMEM)
SMEM = pl.BlockSpec(memory_space=pltpu.SMEM)
HBM = pl.BlockSpec(memory_space=pltpu.HBM)


def call(kernel, outs, scratch, args, flops, specs, out_specs, mib=16):
    return pl.pallas_call(
        kernel,
        out_shape=tuple(jax.ShapeDtypeStruct(s, t) for s, t in outs),
        in_specs=specs,
        out_specs=tuple(out_specs),
        scratch_shapes=scratch,
        compiler_params=pltpu.CompilerParams(vmem_limit_bytes=mib * 2**20),
        cost_estimate=pl.CostEstimate(flops=flops, bytes_accessed=4_000_000, transcendentals=400_000),
    )(*args)


def slab_rows(slabs):
    return -(-2 * 9 * C // (16 * slabs)) * 16


def slab_order(slabs, zh):
    per = C // slabs
    low, rows = (per.bit_length() - 1, slab_rows(slabs))

    def target(n):
        slab = (n & (C - 1)) >> low
        row = (slab >> 1) * rows + (n >> 5) * per + (n & (per - 1))
        return jnp.where((slab & 1) == zh, row, -1)

    return one_hot(slabs // 2 * rows, 2 * 9 * C, target)


def planes(*lead):
    return pltpu.VMEM((*lead, R, W), BF16)


def shaped(*lead):
    return ((*lead, R, W), BF16)


def flat_rows(value):
    return value.reshape(value.shape[0], -1, W)


def one_hot(rows, cols, target):
    row = lax.broadcasted_iota(jnp.int32, (rows, cols), 0)
    col = lax.broadcasted_iota(jnp.int32, (rows, cols), 1)
    return jnp.where(row == target(col), 1.0, 0.0).astype(BF16)


def to_inside():
    return one_hot(2 * R, 2 * R, lambda n: (n & 7) * C + (n >> 3))


def to_outside():
    return one_hot(2 * R, 2 * R, lambda n: (n & (C - 1)) * 8 + (n >> 5))


def reorder(matrix, pieces):
    both = jnp.dot(matrix, jnp.concatenate(pieces, axis=1), preferred_element_type=F32).astype(BF16)
    return [both[:, k * W : (k + 1) * W] for k in range(len(pieces))]


def prepare_kernel(fwd_hbm, acts_hbm, grads_hbm, nat, fwd, acts, grads, sems):
    pairs = ((fwd_hbm, fwd), (acts_hbm, acts), (grads_hbm, grads))
    copies = [pltpu.make_async_copy(src, dst, sems.at[k]) for k, (src, dst) in enumerate(pairs)]
    for copy in copies:
        copy.start()
    order = to_inside()
    for copy in copies:
        copy.wait()
    streams = reorder(order, [acts[0], grads[1], acts[1], grads[0], fwd[1], fwd[0]])
    for k, v in enumerate(streams):
        nat[2 * k] = v[:R]
        nat[2 * k + 1] = v[R:]


def prepare_ends_kernel(flags, batch, loss, first_own, last_own, ends):
    x1, x2, d1, d2 = reorder(to_inside(), [batch[0], batch[1], loss[0], loss[1]])
    for ref, pair in ((first_own, (x1, x2)), (last_own, (d1, d2))):
        for k in range(2):
            ref[k, 0] = pair[k][:R]
            ref[k, 1] = pair[k][R:]
    first = flags[5] == 1

    @pl.when(first)
    def _():
        ends[...] = first_own[...]

    @pl.when(jnp.logical_not(first))
    def _():
        ends[...] = last_own[...]


def matrices(flat):
    k = flat.reshape(2, C, C, 3, 3, 3)
    turned = jnp.flip(k, (3, 4, 5)).transpose(0, 2, 1, 3, 4, 5)
    both = jnp.concatenate([k, turned])
    rows = both.transpose(0, 5, 1, 3, 4, 2)
    rows = jnp.pad(rows, ((0, 0), (0, 0), (0, 0), (0, 0), (0, 1), (0, 0))).reshape(4, 3, C, 3 * R)
    (out,) = call(bands_kernel, [((4, 3 * R, 3 * R), BF16)], [], (rows,), 1_000_000, [VMEM], [VMEM])
    return out


def local(fwd_in, back_out, back_grad, batch_next, loss_grad, weights):
    seg = lax.axis_index("segment")
    slab = lax.axis_index("slab")
    count = lax.axis_size("segment")
    slabs = lax.axis_size("slab")
    ny = slabs // 2
    y, zh = (slab // 2, slab % 2)
    scale = float(fwd_in.shape[3] * slabs * fwd_in.shape[4] * fwd_in.shape[5]) ** (-0.5)

    def route(value, to):
        pairs = []
        for s in range(count):
            for yy in range(ny):
                for zz in range(2):
                    target = to(s, yy, zz)
                    if target is None:
                        continue
                    ts, ty, tz = target
                    if 0 <= ts < count and 0 <= ty < ny:
                        pairs.append((s * slabs + 2 * yy + zz, ts * slabs + 2 * ty + tz))
        return lax.ppermute(value, ("segment", "slab"), pairs)

    def fwd_side(s, zz):
        return 1 - zz if s % SNAKE == SNAKE - 1 and s < count - 1 else zz

    def back_side(s, zz):
        return 1 - zz if s % SNAKE == 0 and s > 0 else zz

    fz = jnp.where((seg % SNAKE == SNAKE - 1) & (seg < count - 1), 1 - zh, zh)
    is_first, is_last = (seg == 0, seg == count - 1)

    def swap(value):
        return route(value, lambda s, yy, zz: (s, yy, 1 - zz))

    def as_flags(*values):
        return jnp.stack([jnp.asarray(v).astype(jnp.int32) for v in values])

    from_first, from_last = (14 % count, (count - 15) % count)
    flags1 = as_flags(zh, y > 0, y < ny - 1, fz, 0, seg == from_first, is_last)
    flags2 = as_flags(zh, (y > 0) | (zh == 1), (y < ny - 1) | (zh == 0), is_first, is_last)
    (nat,) = call(
        prepare_kernel,
        [shaped(12)],
        [pltpu.VMEM((2, 2 * R, W), BF16)] * 3 + [pltpu.SemaphoreType.DMA((3,))],
        (flat_rows(fwd_in[0]), flat_rows(back_out[0]), flat_rows(back_grad[0])),
        100_000_000,
        [HBM] * 3,
        [VMEM],
        58,
    )
    swp = swap(nat)
    first_own, last_own, ends = call(
        prepare_ends_kernel,
        [shaped(2, 2)] * 3,
        [],
        (flags1, flat_rows(batch_next), flat_rows(loss_grad[0])),
        100_000_000,
        [SMEM] + [VMEM] * 2,
        [VMEM] * 3,
    )

    own_planes, ends = lax.optimization_barrier((nat, ends))
    near = route(own_planes, lambda s, yy, zz: (s, yy - 1 + 2 * zz, zz))

    def end_of(s):
        return 0 if s == from_first else count - 1 if s == from_last else -1

    sp1 = route(ends, lambda s, yy, zz: (end_of(s), yy, 1 - zz))
    sp2 = route(ends, lambda s, yy, zz: (end_of(s), yy + (1 if zz == 1 else -1), 1 - zz))
    sp3 = route(last_own, lambda s, yy, zz: (count - 1 if s == count - 2 else -1, yy - 1 + 2 * zz, zz))
    mats = matrices(weights[0])


    swp, near, sp1, sp2, sp3, mats = lax.optimization_barrier((swp, near, sp1, sp2, sp3, mats))

    far = route(swp, lambda s, yy, zz: (s, yy + 1 - 2 * zz, zz))
    bm, bl, bh, dw = call(
        tick1_back,
        [shaped(20), shaped(4), shaped(4), ((2, 9 * C, 3 * C), F32)],
        [planes(8), planes(6), planes(8), planes(6), planes(6), planes(4), planes(6), planes(4), planes(8), planes(6)],
        (flags1, mats, nat, swp, near, far),
        2_000_000_000,
        [SMEM] + [VMEM] * 5,
        [VMEM] * 4,
    )

    def fwd_diag(s, yy, zz):
        r = fwd_side(s, zz)
        return (s + 1, yy + 1 - 2 * r, r)

    bm2 = route(bm, lambda s, yy, zz: (s - 1, yy, back_side(s, zz)))
    bl2 = route(bl, lambda s, yy, zz: (s - 1, yy + 1, back_side(s, zz)))
    bh2 = route(bh, lambda s, yy, zz: (s - 1, yy - 1, back_side(s, zz)))

    fm, fd, ll, lh, y1w = call(
        tick1_forward,
        [shaped(8), shaped(2), shaped(2), shaped(2), shaped(10)],
        [planes(8), planes(6), planes(6), planes(4), planes(8), planes(6)],
        (flags1, mats, nat, swp, near, far, last_own),
        1_000_000_000,
        [SMEM] + [VMEM] * 6,
        [VMEM] * 5,
    )
    ll2 = route(ll, lambda s, yy, zz: (s if s == count - 1 else -1, yy + 1, zz))
    lh2 = route(lh, lambda s, yy, zz: (s if s == count - 1 else -1, yy - 1, zz))
    fd2 = route(fd, fwd_diag)
    fm2 = route(fm, lambda s, yy, zz: (s + 1, yy, fwd_side(s, zz)))

    bm2, bl2, bh2, fm2, fd2, ll2, lh2 = lax.optimization_barrier((bm2, bl2, bh2, fm2, fd2, ll2, lh2))
    out_b, parts = call(
        functools.partial(tick2_back, scale),
        [((4, 2 * R, W), BF16), ((ny, slab_rows(slabs), W), BF16)],
        [planes(8), planes(6), planes(8), planes(6), planes(6), planes(4), planes(6), planes(4), planes(8), planes(6)],
        (flags1, mats, bm2, bl2, bh2, sp1, sp2, sp3, y1w, fm, ll2, lh2, dw),
        1_500_000_000,
        [SMEM] + [VMEM] * 12,
        [VMEM, VMEM],
    )
    back = route(out_b, lambda s, yy, zz: (s - 1, yy, zz))
    columns = [[2 * k + j for k in range(ny)] for j in range(2)]
    parts = lax.all_to_all(parts, "slab", 0, 0, axis_index_groups=columns, tiled=True)

    fm2, out_b = lax.optimization_barrier((fm2, out_b))
    (out_f,) = call(
        tick2_forward,
        [((2, 2 * R, W), BF16)],
        [planes(6), planes(4), planes(4), planes(2), planes(6), planes(4)],
        (flags2, mats, fm2, fd2, sp1, sp2, first_own),
        700_000_000,
        [SMEM] + [VMEM] * 6,
        [VMEM],
    )

    total = jnp.sum(wide(parts), axis=0)[: 2 * 9 * (C // slabs), : 3 * C]
    total = total.reshape(2, 9, C // slabs, 3, C).transpose(0, 4, 2, 1, 3).reshape(1, 2, C, -1)

    acts = jnp.where(is_last, out_f, back[:2])
    grads = jnp.where(is_last, flat_rows(loss_grad[1]), back[2:])
    return (*(v.reshape(fwd_in.shape) for v in (out_f, acts, grads)), total)


def solution(mesh):
    placed = (
        P("segment", None, None, "slab", None, None),
        P("segment", None, None, "slab", None, None),
        P("segment", None, None, "slab", None, None),
        P(None, None, "slab", None, None),
        P(None, None, None, "slab", None, None),
        P("segment", None, None, None),
    )
    return jax.shard_map(
        local,
        mesh=mesh,
        in_specs=placed,
        out_specs=(
            P("segment", None, None, "slab", None, None),
            P("segment", None, None, "slab", None, None),
            P("segment", None, None, "slab", None, None),
            P("segment", None, None, "slab"),
        ),
        check_vma=False,
    )
```

```python
import functools

import jax
import jax.numpy as jnp
from jax import lax
from jax.experimental import pallas as pl
from jax.experimental.pallas import tpu as pltpu
from jax.sharding import PartitionSpec as P

F32 = jnp.float32
BF16 = jnp.bfloat16
C = 32
H = 4
R = C * H
W = 128
SNAKE = 16


def wide(v):
    return v.astype(F32)


def silu(v):
    v = wide(v)
    return (v / (1.0 + jnp.exp(-v))).astype(BF16)


def slope(v):
    v = wide(v)
    sig = 1.0 / (1.0 + jnp.exp(-v))
    return sig * (1.0 + v * (1.0 - sig))


def conv_planes(w_ref, field, start, count, use):
    lane = lax.broadcasted_iota(jnp.int32, (R, W), 1)
    for d in range(0, count, 2):
        n = min(2, count - d)
        x = jnp.concatenate(
            [jnp.concatenate([field[start + d + k + a] for a in range(3)], axis=0) for k in range(n)], axis=1
        )
        y = jnp.dot(w_ref[...], x, preferred_element_type=F32)
        for k in range(n):
            cols = slice(k * W, (k + 1) * W)
            left = jnp.where(lane >= 1, pltpu.roll(y[:R, cols], 1, 1), 0.0)
            right = jnp.where(lane < W - 1, pltpu.roll(y[2 * R :, cols], W - 1, 1), 0.0)
            use(start + d + k, y[R : 2 * R, cols] + left + right)


def mask(d, v, inner, keep, edge=1):
    if d < edge:
        v = v * keep[0]
    if d >= inner - edge:
        v = v * keep[1]
    return v


def forward(n, keep, w_ref, fb, fa, out_a, out_b, act_b, act_a):
    inner = n - 2
    for p in range(n):
        act_b[p] = silu(fb[p])

    def one(d, v):
        out = mask(d, wide(fa[d]) + v, inner, keep, max(1, n - 8)).astype(BF16)
        out_a[d] = out
        act_a[d] = silu(out)

    conv_planes(w_ref.at[0], act_b, 0, inner, one)

    def two(d, v):
        out_b[d] = (wide(fb[d + 2]) + v).astype(BF16)

    conv_planes(w_ref.at[1], act_a, 0, inner - 2, two)


def backward(keep, w_ref, bb, ba, db, da, rec_a, rec_b, grad_a, grad_b, act_b, act_a, first, count):
    n, inner = (8, 6)
    for p in range(n):
        act_b[p] = silu(bb[p])

    def one(d, v):
        out = mask(d, wide(ba[d]) - v, inner, keep).astype(BF16)
        rec_a[d] = out
        act_a[d] = silu(out)

    conv_planes(w_ref.at[1], act_b, 0, inner, one)

    def two(d, v):
        grad_a[d] = mask(d, wide(da[d]) + slope(bb[d + 1]) * v, inner, keep).astype(BF16)

    conv_planes(w_ref.at[3], db, 0, inner, two)

    def three(d, v):
        rec_b[d] = (wide(bb[d + 2]) - v).astype(BF16)

    conv_planes(w_ref.at[0], act_a, first, count, three)

    def four(d, v):
        grad_b[d] = (wide(db[d + 2]) + slope(rec_a[d + 1]) * v).astype(BF16)

    conv_planes(w_ref.at[2], grad_a, first, count, four)


def move(pairs):
    for src, dst in pairs:
        for k in range(dst.shape[0]):
            dst[k] = src[k]


def at(ref, first, count):
    return ref.at[pl.ds(first, count)]


def window1(zh, b, a, nat_b, nat_a, swp_b, swp_a, near_b, near_a, far_b, far_a):
    return [
        (nat_b, at(b, 2 + 2 * zh, 2)),
        (swp_b, at(b, 4 - 2 * zh, 2)),
        (near_b, at(b, 6 - 6 * zh, 2)),
        (far_b, at(b, 6 * zh, 2)),
        (nat_a, at(a, 1 + 2 * zh, 2)),
        (swp_a, at(a, 3 - 2 * zh, 2)),
        (near_a, at(a, 5 - 5 * zh, 1)),
        (far_a, at(a, 5 * zh, 1)),
    ]


def special(zh, b, a, own, sp1, sp2):
    return [
        (own[1], at(b, 2, 2)),
        (sp1.at[1], at(b, 4 - 4 * zh, 2)),
        (sp2.at[1], at(b, 4 * zh, 2)),
        (own[0], at(a, 1, 2)),
        (at(sp1.at[0], zh, 1), at(a, 3 - 3 * zh, 1)),
        (at(sp2.at[0], 1 - zh, 1), at(a, 3 * zh, 1)),
    ]


def keeps(flags):
    return (flags[1].astype(F32), flags[2].astype(F32))


def weight_sums(db, grad_a, act_b, act_a):
    return (
        wgrad_pair(at(grad_a, 1, 4), act_a),
        wgrad_pair(at(db, 2, 4), at(act_b, 1, 6)),
    )


def tick1_window(zh, b, a, b_at, a_at, near_b, near_a, nat, swp, near, far):
    move(
        window1(
            zh, b, a, at(nat, b_at, 2), at(nat, a_at, 2), at(swp, b_at, 2), at(swp, a_at, 2),
            at(near, near_b, 2), at(near, near_a, 1), at(far, b_at, 2), at(far, a_at + 1 - zh, 1),
        )
    )


def tick1_back(flags, w_ref, nat, swp, near, far, bm, bl, bh, dw, *scratch):
    bb, ba, db, da, rec_a, rec_b, grad_a, grad_b, act_b, act_a = scratch
    for k, (b, a) in enumerate(((bb, ba), (db, da))):
        tick1_window(flags[0], b, a, 2 * k, 4 + 2 * k, 2 * k, 8 + k, nat, swp, near, far)
    backward(keeps(flags), w_ref, bb, ba, db, da, rec_a, rec_b, grad_a, grad_b, act_b, act_a, 0, 4)
    move([
        (rec_b, at(bm, 0, 4)),
        (grad_b, at(bm, 4, 4)),
        (rec_a, at(bm, 8, 6)),
        (grad_a, at(bm, 14, 6)),
        (at(rec_b, 2, 2), at(bl, 0, 2)),
        (at(grad_b, 2, 2), at(bl, 2, 2)),
        (at(rec_b, 0, 2), at(bh, 0, 2)),
        (at(grad_b, 0, 2), at(bh, 2, 2)),
    ])
    dw[0], dw[1] = weight_sums(db, grad_a, act_b, act_a)


def tick1_forward(flags, w_ref, nat, swp, near, far, last_own, e1, e2, fm, fd, own, *scratch):
    fb, fa, out_a, out_b, act_b, act_a = scratch
    zh, fz = (flags[0], flags[3])

    @pl.when(flags[6] == 0)
    def _():
        tick1_window(zh, fb, fa, 8, 10, 4, 6 + zh, nat, swp, near, far)
        forward(8, keeps(flags), w_ref, fb, fa, out_a, out_b, act_b, act_a)
        move([
            (at(out_b, 0, 4), at(fm, 0, 4)),
            (at(out_a, 2 * fz, 4), at(fm, 4, 4)),
            (at(out_b, 2 - 2 * fz, 2), fd),
        ])

    @pl.when(flags[6] == 1)
    def _():
        for win, k in ((at(fb, 1, 8), 8), (fa, 10)):
            move([
                (at(nat, k, 2), at(win, 2 + 2 * zh, 2)),
                (at(swp, k, 2), at(win, 4 - 2 * zh, 2)),
                (at(near, k - 4, 2), at(win, 6 - 6 * zh, 2)),
                (at(far, k, 2), at(win, 6 * zh, 2)),
            ])
        move([(at(e1, 1 - zh, 1), at(fb, 9 * zh, 1)), (at(e2, zh, 1), at(fb, 9 - 9 * zh, 1))])
        forward(10, keeps(flags), w_ref, fb, fa, out_a, out_b, act_b, act_a)
        move([
            (out_a, at(own, 0, 8)),
            (out_b, at(own, 8, 6)),
            (last_own.at[0], at(own, 14, 2)),
            (last_own.at[1], at(own, 16, 2)),
        ])


def tick2_back(
    scale, flags, w_ref, bm, bl, bh, sp1, sp2, sp3, own, dw, out, parts, *scratch
):
    bb, ba, db, da, rec_a, rec_b, grad_a, grad_b, act_b, act_a = scratch
    zh = flags[0]

    @pl.when(flags[6] == 1)
    def _():
        move(window1(
            zh, db, da, at(own, 16, 2), at(own, 14, 2), sp1.at[1], sp1.at[0],
            sp3.at[1], at(sp3.at[0], zh, 1), sp2.at[1], at(sp2.at[0], 1 - zh, 1),
        ))
        move([
            (at(own, 0, 8), bb),
            (at(own, 8, 6), ba),
        ])

    @pl.when(flags[6] == 0)
    def _():
        move([
            (at(bl, 0, 2), at(bb, 0, 2)),
            (at(bm, 0, 4), at(bb, 2, 4)),
            (at(bh, 0, 2), at(bb, 6, 2)),
            (at(bl, 2, 2), at(db, 0, 2)),
            (at(bm, 4, 4), at(db, 2, 4)),
            (at(bh, 2, 2), at(db, 6, 2)),
            (at(bm, 8, 6), ba),
            (at(bm, 14, 6), da),
        ])

    order, back_order = (slab_order(2 * parts.shape[0], zh), to_outside())
    backward(keeps(flags), w_ref, bb, ba, db, da, rec_a, rec_b, grad_a, grad_b, act_b, act_a, 2 * zh, 2)
    own_a, own_b = (pl.ds(1 + 2 * zh, 2), pl.ds(2 * zh, 2))
    pieces = [rec_b[own_b], rec_a[own_a], grad_a[own_a], grad_b[own_b]]
    for k, v in enumerate(reorder(back_order, [p.reshape(2 * R, W) for p in pieces])):
        out[k] = v
    sums = [dw[k] + v for k, v in enumerate(weight_sums(db, grad_a, act_b, act_a))]
    sums = jnp.concatenate([(v * scale).astype(BF16) for v in sums], axis=0)
    ordered = jnp.dot(order, sums, preferred_element_type=F32).astype(BF16)
    parts[:, :, : 3 * C] = ordered.reshape(*parts.shape[:2], 3 * C)
    parts[:, :, 3 * C :] = jnp.zeros((*parts.shape[:2], W - 3 * C), BF16)


def tick2_forward(flags, w_ref, fm, fd, sp1, sp2, first_own, out, *scratch):
    fb, fa, out_a, out_b, act_b, act_a = scratch
    zh, first = (flags[0], flags[3])

    @pl.when(first == 1)
    def _():
        move(special(zh, fb, fa, (first_own.at[0], first_own.at[1]), sp1, sp2))

    @pl.when(first == 0)
    def _():
        move([(at(fm, 0, 4), at(fb, 2 - 2 * zh, 4)), (fd, at(fb, 4 * zh, 2)), (at(fm, 4, 4), fa)])

    forward(6, keeps(flags), w_ref, fb, fa, out_a, out_b, act_b, act_a)
    for k, v in enumerate(reorder(to_outside(), [p.reshape(2 * R, W) for p in (out_a[1:3], out_b[...])])):
        out[k] = v


def wgrad_pair(g_ref, u_ref):
    lane = lax.broadcasted_iota(jnp.int32, (C, W), 1)
    zero = jnp.zeros((C, W), BF16)
    left, right = ([], [])
    for d in range(g_ref.shape[0]):
        for h in range(H):
            g = wide(g_ref[d, h * C : (h + 1) * C])
            down = jnp.where(lane < W - 1, pltpu.roll(g, W - 1, 1), 0.0)
            up = jnp.where(lane >= 1, pltpu.roll(g, 1, 1), 0.0)
            left.append(jnp.concatenate([down, g, up], axis=0).astype(BF16))
            rows = []
            for a in range(3):
                for b in range(3):
                    at = h + b - 1
                    rows.append(u_ref[d + a, at * C : (at + 1) * C] if 0 <= at < H else zero)
            right.append(jnp.concatenate(rows, axis=0))
    return lax.dot_general(
        jnp.concatenate(right, axis=1),
        jnp.concatenate(left, axis=1),
        (((1,), (1,)), ((), ())),
        preferred_element_type=F32,
    )


def bands_kernel(rows, out):
    lane = lax.broadcasted_iota(jnp.int32, (C, R), 1)
    for kind in range(4):
        for c in range(3):
            for a in range(3):
                tile = wide(rows[kind, c, :, a * R : (a + 1) * R])
                for h in range(H):
                    moved = tile if h == 1 else pltpu.roll(tile, ((h - 1) * C) % R, 1)
                    if h == 0:
                        moved = jnp.where(lane < 2 * C, moved, 0.0)
                    if h == 3:
                        moved = jnp.where(lane >= 2 * C, moved, 0.0)
                    at_row = (c * H + h) * C
                    out[kind, at_row : at_row + C, a * R : (a + 1) * R] = moved.astype(BF16)


VMEM = pl.BlockSpec(memory_space=pltpu.VMEM)
SMEM = pl.BlockSpec(memory_space=pltpu.SMEM)
HBM = pl.BlockSpec(memory_space=pltpu.HBM)


def call(kernel, outs, scratch, args, flops, specs, out_specs, mib=16):
    return pl.pallas_call(
        kernel,
        out_shape=tuple(jax.ShapeDtypeStruct(s, t) for s, t in outs),
        in_specs=specs,
        out_specs=tuple(out_specs),
        scratch_shapes=scratch,
        compiler_params=pltpu.CompilerParams(vmem_limit_bytes=mib * 2**20),
        cost_estimate=pl.CostEstimate(flops=flops, bytes_accessed=4_000_000, transcendentals=400_000),
    )(*args)


def slab_rows(slabs):
    return -(-2 * 9 * C // (16 * slabs)) * 16


def slab_order(slabs, zh):
    per = C // slabs
    low, rows = (per.bit_length() - 1, slab_rows(slabs))

    def target(n):
        slab = (n & (C - 1)) >> low
        row = (slab >> 1) * rows + (n >> 5) * per + (n & (per - 1))
        return jnp.where((slab & 1) == zh, row, -1)

    return one_hot(slabs // 2 * rows, 2 * 9 * C, target)


def planes(*lead):
    return pltpu.VMEM((*lead, R, W), BF16)


def shaped(*lead):
    return ((*lead, R, W), BF16)


def flat_rows(value):
    return value.reshape(value.shape[0], -1, W)


def one_hot(rows, cols, target):
    row = lax.broadcasted_iota(jnp.int32, (rows, cols), 0)
    col = lax.broadcasted_iota(jnp.int32, (rows, cols), 1)
    return jnp.where(row == target(col), 1.0, 0.0).astype(BF16)


def to_inside():
    return one_hot(2 * R, 2 * R, lambda n: (n & 7) * C + (n >> 3))


def to_outside():
    return one_hot(2 * R, 2 * R, lambda n: (n & (C - 1)) * 8 + (n >> 5))


def reorder(matrix, pieces):
    both = jnp.dot(matrix, jnp.concatenate(pieces, axis=1), preferred_element_type=F32).astype(BF16)
    return [both[:, k * W : (k + 1) * W] for k in range(len(pieces))]


def prepare_kernel(fwd_hbm, acts_hbm, grads_hbm, nat, fwd, acts, grads, sems):
    pairs = ((fwd_hbm, fwd), (acts_hbm, acts), (grads_hbm, grads))
    copies = [pltpu.make_async_copy(src, dst, sems.at[k]) for k, (src, dst) in enumerate(pairs)]
    for copy in copies:
        copy.start()
    order = to_inside()
    for copy in copies:
        copy.wait()
    streams = reorder(order, [acts[0], grads[1], acts[1], grads[0], fwd[1], fwd[0]])
    for k, v in enumerate(streams):
        nat[2 * k] = v[:R]
        nat[2 * k + 1] = v[R:]


def prepare_ends_kernel(flags, batch, loss, nat, first_own, last_own, ends, near, nat_x2):
    zh = flags[0]
    move([
        (at(nat, 0, 4), at(near, 0, 4)),
        (at(nat, 8, 4), at(near, 4, 4)),
        (at(nat, 4 + zh, 1), at(near, 8, 1)),
        (at(nat, 6 + zh, 1), at(near, 9, 1)),
        (at(nat, 8, 2), nat_x2),
    ])
    x1, x2, d1, d2 = reorder(to_inside(), [batch[0], batch[1], loss[0], loss[1]])
    for ref, pair in ((first_own, (x1, x2)), (last_own, (d1, d2))):
        for k in range(2):
            ref[k, 0] = pair[k][:R]
            ref[k, 1] = pair[k][R:]
    first = flags[5] == 1

    @pl.when(first)
    def _():
        ends[...] = first_own[...]

    @pl.when(jnp.logical_not(first))
    def _():
        ends[...] = last_own[...]


def matrices(flat):
    k = flat.reshape(2, C, C, 3, 3, 3)
    turned = jnp.flip(k, (3, 4, 5)).transpose(0, 2, 1, 3, 4, 5)
    both = jnp.concatenate([k, turned])
    rows = both.transpose(0, 5, 1, 3, 4, 2)
    rows = jnp.pad(rows, ((0, 0), (0, 0), (0, 0), (0, 0), (0, 1), (0, 0))).reshape(4, 3, C, 3 * R)
    (out,) = call(bands_kernel, [((4, 3 * R, 3 * R), BF16)], [], (rows,), 1_000_000, [VMEM], [VMEM])
    return out


def local(fwd_in, back_out, back_grad, batch_next, loss_grad, weights):
    seg = lax.axis_index("segment")
    slab = lax.axis_index("slab")
    count = lax.axis_size("segment")
    slabs = lax.axis_size("slab")
    ny = slabs // 2
    y, zh = (slab // 2, slab % 2)
    scale = float(fwd_in.shape[3] * slabs * fwd_in.shape[4] * fwd_in.shape[5]) ** (-0.5)

    def route(value, to):
        pairs = []
        for s in range(count):
            for yy in range(ny):
                for zz in range(2):
                    target = to(s, yy, zz)
                    if target is None:
                        continue
                    ts, ty, tz = target
                    if 0 <= ts < count and 0 <= ty < ny:
                        pairs.append((s * slabs + 2 * yy + zz, ts * slabs + 2 * ty + tz))
        return lax.ppermute(value, ("segment", "slab"), pairs)

    def fwd_side(s, zz):
        return 1 - zz if s % SNAKE == SNAKE - 1 and s < count - 1 else zz

    def back_side(s, zz):
        return 1 - zz if s % SNAKE == 0 and s > 0 else zz

    fz = jnp.where((seg % SNAKE == SNAKE - 1) & (seg < count - 1), 1 - zh, zh)
    is_first, is_last = (seg == 0, seg == count - 1)

    def swap(value):
        return route(value, lambda s, yy, zz: (s, yy, 1 - zz))

    def as_flags(*values):
        return jnp.stack([jnp.asarray(v).astype(jnp.int32) for v in values])

    from_first, from_last = (14 % count, (count - 15) % count)
    flags1 = as_flags(zh, y > 0, y < ny - 1, fz, 0, seg == from_first, is_last)
    flags2 = as_flags(zh, (y > 0) | (zh == 1), (y < ny - 1) | (zh == 0), is_first, is_last)
    (nat,) = call(
        prepare_kernel,
        [shaped(12)],
        [pltpu.VMEM((2, 2 * R, W), BF16)] * 3 + [pltpu.SemaphoreType.DMA((3,))],
        (flat_rows(fwd_in[0]), flat_rows(back_out[0]), flat_rows(back_grad[0])),
        100_000_000,
        [HBM] * 3,
        [VMEM],
        58,
    )
    swp = swap(nat)
    first_own, last_own, ends, near, nat_x2 = call(
        prepare_ends_kernel,
        [shaped(2, 2)] * 3 + [shaped(10), shaped(2)],
        [],
        (flags1, flat_rows(batch_next), flat_rows(loss_grad[0]), nat),
        100_000_000,
        [SMEM] + [VMEM] * 3,
        [VMEM] * 5,
    )

    near = route(near, lambda s, yy, zz: (s, yy - 1 + 2 * zz, zz))
    e1 = route(nat_x2, lambda s, yy, zz: (s if s == count - 1 else -1, yy + 1 - 2 * zz, zz))
    e2 = route(nat_x2, lambda s, yy, zz: (s if s == count - 1 else -1, yy + 1 - 2 * zz, 1 - zz))

    def end_of(s):
        return 0 if s == from_first else count - 1 if s == from_last else -1

    sp1 = route(ends, lambda s, yy, zz: (end_of(s), yy, 1 - zz))
    sp2 = route(ends, lambda s, yy, zz: (end_of(s), yy + (1 if zz == 1 else -1), 1 - zz))
    sp3 = route(last_own, lambda s, yy, zz: (count - 1 if s == count - 2 else -1, yy - 1 + 2 * zz, zz))
    mats = matrices(weights[0])


    swp, near, sp1, sp2, sp3, e1, e2, mats = lax.optimization_barrier((swp, near, sp1, sp2, sp3, e1, e2, mats))

    far = route(swp, lambda s, yy, zz: (s, yy + 1 - 2 * zz, zz))
    bm, bl, bh, dw = call(
        tick1_back,
        [shaped(20), shaped(4), shaped(4), ((2, 9 * C, 3 * C), F32)],
        [planes(8), planes(6), planes(8), planes(6), planes(6), planes(4), planes(6), planes(4), planes(8), planes(6)],
        (flags1, mats, nat, swp, near, far),
        2_000_000_000,
        [SMEM] + [VMEM] * 5,
        [VMEM] * 4,
    )

    def fwd_diag(s, yy, zz):
        r = fwd_side(s, zz)
        return (s + 1, yy + 1 - 2 * r, r)

    bm2 = route(bm, lambda s, yy, zz: (s - 1, yy, back_side(s, zz)))
    bl2 = route(bl, lambda s, yy, zz: (s - 1, yy + 1, back_side(s, zz)))
    bh2 = route(bh, lambda s, yy, zz: (s - 1, yy - 1, back_side(s, zz)))

    fm, fd, own = call(
        tick1_forward,
        [shaped(8), shaped(2), shaped(18)],
        [planes(10), planes(8), planes(8), planes(6), planes(10), planes(8)],
        (flags1, mats, nat, swp, near, far, last_own, e1, e2),
        1_000_000_000,
        [SMEM] + [VMEM] * 8,
        [VMEM] * 3,
    )
    fd2 = route(fd, fwd_diag)
    fm2 = route(fm, lambda s, yy, zz: (s + 1, yy, fwd_side(s, zz)))

    bm2, bl2, bh2, fm2, fd2 = lax.optimization_barrier((bm2, bl2, bh2, fm2, fd2))
    out_b, parts = call(
        functools.partial(tick2_back, scale),
        [((4, 2 * R, W), BF16), ((ny, slab_rows(slabs), W), BF16)],
        [planes(8), planes(6), planes(8), planes(6), planes(6), planes(4), planes(6), planes(4), planes(8), planes(6)],
        (flags1, mats, bm2, bl2, bh2, sp1, sp2, sp3, own, dw),
        1_500_000_000,
        [SMEM] + [VMEM] * 9,
        [VMEM, VMEM],
    )
    back = route(out_b, lambda s, yy, zz: (s - 1, yy, zz))
    columns = [[2 * k + j for k in range(ny)] for j in range(2)]
    parts = lax.all_to_all(parts, "slab", 0, 0, axis_index_groups=columns, tiled=True)

    fm2, out_b = lax.optimization_barrier((fm2, out_b))
    (out_f,) = call(
        tick2_forward,
        [((2, 2 * R, W), BF16)],
        [planes(6), planes(4), planes(4), planes(2), planes(6), planes(4)],
        (flags2, mats, fm2, fd2, sp1, sp2, first_own),
        700_000_000,
        [SMEM] + [VMEM] * 6,
        [VMEM],
    )

    total = jnp.sum(wide(parts), axis=0)[: 2 * 9 * (C // slabs), : 3 * C]
    total = total.reshape(2, 9, C // slabs, 3, C).transpose(0, 4, 2, 1, 3).reshape(1, 2, C, -1)

    acts = jnp.where(is_last, out_f, back[:2])
    grads = jnp.where(is_last, flat_rows(loss_grad[1]), back[2:])
    return (*(v.reshape(fwd_in.shape) for v in (out_f, acts, grads)), total)


def solution(mesh):
    placed = (
        P("segment", None, None, "slab", None, None),
        P("segment", None, None, "slab", None, None),
        P("segment", None, None, "slab", None, None),
        P(None, None, "slab", None, None),
        P(None, None, None, "slab", None, None),
        P("segment", None, None, None),
    )
    return jax.shard_map(
        local,
        mesh=mesh,
        in_specs=placed,
        out_specs=(
            P("segment", None, None, "slab", None, None),
            P("segment", None, None, "slab", None, None),
            P("segment", None, None, "slab", None, None),
            P("segment", None, None, "slab"),
        ),
        check_vma=False,
    )
```

```python
import functools

import jax
import jax.numpy as jnp
from jax import lax
from jax.experimental import pallas as pl
from jax.experimental.pallas import tpu as pltpu
from jax.sharding import PartitionSpec as P

F32 = jnp.float32
BF16 = jnp.bfloat16
C = 32
H = 4
R = C * H
W = 128
SNAKE = 16


def wide(v):
    return v.astype(F32)


def silu(v):
    v = wide(v)
    return (v / (1.0 + jnp.exp(-v))).astype(BF16)


def slope(v):
    v = wide(v)
    sig = 1.0 / (1.0 + jnp.exp(-v))
    return sig * (1.0 + v * (1.0 - sig))


def conv_planes(w_ref, field, start, count, use):
    lane = lax.broadcasted_iota(jnp.int32, (R, W), 1)
    for d in range(0, count, 2):
        n = min(2, count - d)
        x = jnp.concatenate(
            [jnp.concatenate([field[start + d + k + a] for a in range(3)], axis=0) for k in range(n)], axis=1
        )
        y = jnp.dot(w_ref[...], x, preferred_element_type=F32)
        for k in range(n):
            cols = slice(k * W, (k + 1) * W)
            left = jnp.where(lane >= 1, pltpu.roll(y[:R, cols], 1, 1), 0.0)
            right = jnp.where(lane < W - 1, pltpu.roll(y[2 * R :, cols], W - 1, 1), 0.0)
            use(start + d + k, y[R : 2 * R, cols] + left + right)


def mask(d, v, inner, keep, edge=1):
    if d < edge:
        v = v * keep[0]
    if d >= inner - edge:
        v = v * keep[1]
    return v


def forward(n, keep, w_ref, fb, fa, out_a, out_b, act_b, act_a):
    inner = n - 2
    for p in range(n):
        act_b[p] = silu(fb[p])

    def one(d, v):
        out = mask(d, wide(fa[d]) + v, inner, keep, max(1, n - 8)).astype(BF16)
        out_a[d] = out
        act_a[d] = silu(out)

    conv_planes(w_ref.at[0], act_b, 0, inner, one)

    def two(d, v):
        out_b[d] = (wide(fb[d + 2]) + v).astype(BF16)

    conv_planes(w_ref.at[1], act_a, 0, inner - 2, two)


def backward(keep, w_ref, bb, ba, db, da, rec_a, rec_b, grad_a, grad_b, act_b, act_a, first, count):
    n, inner = (8, 6)
    for p in range(n):
        act_b[p] = silu(bb[p])

    def one(d, v):
        out = mask(d, wide(ba[d]) - v, inner, keep).astype(BF16)
        rec_a[d] = out
        act_a[d] = silu(out)

    conv_planes(w_ref.at[1], act_b, 0, inner, one)

    def two(d, v):
        grad_a[d] = mask(d, wide(da[d]) + slope(bb[d + 1]) * v, inner, keep).astype(BF16)

    conv_planes(w_ref.at[3], db, 0, inner, two)

    def three(d, v):
        rec_b[d] = (wide(bb[d + 2]) - v).astype(BF16)

    conv_planes(w_ref.at[0], act_a, first, count, three)

    def four(d, v):
        grad_b[d] = (wide(db[d + 2]) + slope(rec_a[d + 1]) * v).astype(BF16)

    conv_planes(w_ref.at[2], grad_a, first, count, four)


def move(pairs):
    for src, dst in pairs:
        for k in range(dst.shape[0]):
            dst[k] = src[k]


def at(ref, first, count):
    return ref.at[pl.ds(first, count)]


def window1(zh, b, a, nat_b, nat_a, swp_b, swp_a, near_b, near_a, far_b, far_a):
    return [
        (nat_b, at(b, 2 + 2 * zh, 2)),
        (swp_b, at(b, 4 - 2 * zh, 2)),
        (near_b, at(b, 6 - 6 * zh, 2)),
        (far_b, at(b, 6 * zh, 2)),
        (nat_a, at(a, 1 + 2 * zh, 2)),
        (swp_a, at(a, 3 - 2 * zh, 2)),
        (near_a, at(a, 5 - 5 * zh, 1)),
        (far_a, at(a, 5 * zh, 1)),
    ]


def special(zh, b, a, own, sp1, sp2):
    return [
        (own[1], at(b, 2, 2)),
        (sp1.at[1], at(b, 4 - 4 * zh, 2)),
        (sp2.at[1], at(b, 4 * zh, 2)),
        (own[0], at(a, 1, 2)),
        (at(sp1.at[0], zh, 1), at(a, 3 - 3 * zh, 1)),
        (at(sp2.at[0], 1 - zh, 1), at(a, 3 * zh, 1)),
    ]


def keeps(flags):
    return (flags[1].astype(F32), flags[2].astype(F32))


def weight_sums(db, grad_a, act_b, act_a):
    return (
        wgrad_pair(at(grad_a, 1, 4), act_a),
        wgrad_pair(at(db, 2, 4), at(act_b, 1, 6)),
    )


def tick1_window(zh, b, a, b_at, a_at, near_b, near_a, nat, swp, near, far):
    move(
        window1(
            zh, b, a, at(nat, b_at, 2), at(nat, a_at, 2), at(swp, b_at, 2), at(swp, a_at, 2),
            at(near, near_b, 2), at(near, near_a, 1), at(far, b_at, 2), at(far, a_at + 1 - zh, 1),
        )
    )


def tick1_back(flags, w_ref, nat, swp, near, far, bm, bl, bh, dw, *scratch):
    bb, ba, db, da, rec_a, rec_b, grad_a, grad_b, act_b, act_a = scratch
    for k, (b, a) in enumerate(((bb, ba), (db, da))):
        tick1_window(flags[0], b, a, 2 * k, 4 + 2 * k, 2 * k, 8 + k, nat, swp, near, far)
    backward(keeps(flags), w_ref, bb, ba, db, da, rec_a, rec_b, grad_a, grad_b, act_b, act_a, 0, 4)
    move([
        (rec_b, at(bm, 0, 4)),
        (grad_b, at(bm, 4, 4)),
        (rec_a, at(bm, 8, 6)),
        (grad_a, at(bm, 14, 6)),
        (at(rec_b, 2, 2), at(bl, 0, 2)),
        (at(grad_b, 2, 2), at(bl, 2, 2)),
        (at(rec_b, 0, 2), at(bh, 0, 2)),
        (at(grad_b, 0, 2), at(bh, 2, 2)),
    ])
    dw[0], dw[1] = weight_sums(db, grad_a, act_b, act_a)


def tick1_forward(flags, w_ref, nat, swp, near, far, last_own, e1, e2, fm, fd, own, *scratch):
    fb, fa, out_a, out_b, act_b, act_a = scratch
    zh, fz = (flags[0], flags[3])

    @pl.when(flags[6] == 0)
    def _():
        tick1_window(zh, fb, fa, 8, 10, 4, 6 + zh, nat, swp, near, far)
        forward(8, keeps(flags), w_ref, fb, fa, out_a, out_b, act_b, act_a)
        move([
            (at(out_b, 0, 4), at(fm, 0, 4)),
            (at(out_a, 2 * fz, 4), at(fm, 4, 4)),
            (at(out_b, 2 - 2 * fz, 2), fd),
        ])

    @pl.when(flags[6] == 1)
    def _():
        for win, k in ((at(fb, 1, 8), 8), (fa, 10)):
            move([
                (at(nat, k, 2), at(win, 2 + 2 * zh, 2)),
                (at(swp, k, 2), at(win, 4 - 2 * zh, 2)),
                (at(near, k - 4, 2), at(win, 6 - 6 * zh, 2)),
                (at(far, k, 2), at(win, 6 * zh, 2)),
            ])
        move([(at(e1, 1 - zh, 1), at(fb, 9 * zh, 1)), (at(e2, zh, 1), at(fb, 9 - 9 * zh, 1))])
        forward(10, keeps(flags), w_ref, fb, fa, out_a, out_b, act_b, act_a)
        move([
            (out_a, at(own, 0, 8)),
            (out_b, at(own, 8, 6)),
            (last_own.at[0], at(own, 14, 2)),
            (last_own.at[1], at(own, 16, 2)),
        ])


def tick2_back(
    scale, flags, w_ref, bm, bl, bh, sp1, sp2, sp3, own, dw, out, parts, *scratch
):
    bb, ba, db, da, rec_a, rec_b, grad_a, grad_b, act_b, act_a = scratch
    zh = flags[0]

    @pl.when(flags[6] == 1)
    def _():
        move(window1(
            zh, db, da, at(own, 16, 2), at(own, 14, 2), sp1.at[1], sp1.at[0],
            sp3.at[1], at(sp3.at[0], zh, 1), sp2.at[1], at(sp2.at[0], 1 - zh, 1),
        ))
        move([
            (at(own, 0, 8), bb),
            (at(own, 8, 6), ba),
        ])

    @pl.when(flags[6] == 0)
    def _():
        move([
            (at(bl, 0, 2), at(bb, 0, 2)),
            (at(bm, 0, 4), at(bb, 2, 4)),
            (at(bh, 0, 2), at(bb, 6, 2)),
            (at(bl, 2, 2), at(db, 0, 2)),
            (at(bm, 4, 4), at(db, 2, 4)),
            (at(bh, 2, 2), at(db, 6, 2)),
            (at(bm, 8, 6), ba),
            (at(bm, 14, 6), da),
        ])

    order, back_order = (slab_order(2 * parts.shape[0], zh), to_outside())
    backward(keeps(flags), w_ref, bb, ba, db, da, rec_a, rec_b, grad_a, grad_b, act_b, act_a, 2 * zh, 2)
    own_a, own_b = (pl.ds(1 + 2 * zh, 2), pl.ds(2 * zh, 2))
    pieces = [rec_b[own_b], rec_a[own_a], grad_a[own_a], grad_b[own_b]]
    for k, v in enumerate(reorder(back_order, [p.reshape(2 * R, W) for p in pieces])):
        out[k] = v
    sums = [dw[k] + v for k, v in enumerate(weight_sums(db, grad_a, act_b, act_a))]
    sums = jnp.concatenate([(v * scale).astype(BF16) for v in sums], axis=0)
    ordered = jnp.dot(order, sums, preferred_element_type=F32).astype(BF16)
    parts[:, :, : 3 * C] = ordered.reshape(*parts.shape[:2], 3 * C)
    parts[:, :, 3 * C :] = jnp.zeros((*parts.shape[:2], W - 3 * C), BF16)


def tick2_forward(flags, w_ref, fm, fd, sp1, sp2, first_own, out, *scratch):
    fb, fa, out_a, out_b, act_b, act_a = scratch
    zh, first = (flags[0], flags[3])

    @pl.when(first == 1)
    def _():
        move(special(zh, fb, fa, (first_own.at[0], first_own.at[1]), sp1, sp2))

    @pl.when(first == 0)
    def _():
        move([(at(fm, 0, 4), at(fb, 2 - 2 * zh, 4)), (fd, at(fb, 4 * zh, 2)), (at(fm, 4, 4), fa)])

    forward(6, keeps(flags), w_ref, fb, fa, out_a, out_b, act_b, act_a)
    for k, v in enumerate(reorder(to_outside(), [p.reshape(2 * R, W) for p in (out_a[1:3], out_b[...])])):
        out[k] = v


def wgrad_pair(g_ref, u_ref):
    lane = lax.broadcasted_iota(jnp.int32, (C, W), 1)
    zero = jnp.zeros((C, W), BF16)
    left, right = ([], [])
    for d in range(g_ref.shape[0]):
        for h in range(H):
            g = wide(g_ref[d, h * C : (h + 1) * C])
            down = jnp.where(lane < W - 1, pltpu.roll(g, W - 1, 1), 0.0)
            up = jnp.where(lane >= 1, pltpu.roll(g, 1, 1), 0.0)
            left.append(jnp.concatenate([down, g, up], axis=0).astype(BF16))
            rows = []
            for a in range(3):
                for b in range(3):
                    at = h + b - 1
                    rows.append(u_ref[d + a, at * C : (at + 1) * C] if 0 <= at < H else zero)
            right.append(jnp.concatenate(rows, axis=0))
    return lax.dot_general(
        jnp.concatenate(right, axis=1),
        jnp.concatenate(left, axis=1),
        (((1,), (1,)), ((), ())),
        preferred_element_type=F32,
    )


def bands_kernel(rows, out):
    lane = lax.broadcasted_iota(jnp.int32, (C, R), 1)
    for kind in range(4):
        for c in range(3):
            for a in range(3):
                tile = wide(rows[kind, c, :, a * R : (a + 1) * R])
                for h in range(H):
                    moved = tile if h == 1 else pltpu.roll(tile, ((h - 1) * C) % R, 1)
                    if h == 0:
                        moved = jnp.where(lane < 2 * C, moved, 0.0)
                    if h == 3:
                        moved = jnp.where(lane >= 2 * C, moved, 0.0)
                    at_row = (c * H + h) * C
                    out[kind, at_row : at_row + C, a * R : (a + 1) * R] = moved.astype(BF16)


VMEM = pl.BlockSpec(memory_space=pltpu.VMEM)
SMEM = pl.BlockSpec(memory_space=pltpu.SMEM)
HBM = pl.BlockSpec(memory_space=pltpu.HBM)


def call(kernel, outs, scratch, args, flops, specs, out_specs, mib=16):
    return pl.pallas_call(
        kernel,
        out_shape=tuple(jax.ShapeDtypeStruct(s, t) for s, t in outs),
        in_specs=specs,
        out_specs=tuple(out_specs),
        scratch_shapes=scratch,
        compiler_params=pltpu.CompilerParams(vmem_limit_bytes=mib * 2**20),
        cost_estimate=pl.CostEstimate(flops=flops, bytes_accessed=4_000_000, transcendentals=400_000),
    )(*args)


def slab_rows(slabs):
    return -(-2 * 9 * C // (16 * slabs)) * 16


def slab_order(slabs, zh):
    per = C // slabs
    low, rows = (per.bit_length() - 1, slab_rows(slabs))

    def target(n):
        slab = (n & (C - 1)) >> low
        row = (slab >> 1) * rows + (n >> 5) * per + (n & (per - 1))
        return jnp.where((slab & 1) == zh, row, -1)

    return one_hot(slabs // 2 * rows, 2 * 9 * C, target)


def planes(*lead):
    return pltpu.VMEM((*lead, R, W), BF16)


def shaped(*lead):
    return ((*lead, R, W), BF16)


def flat_rows(value):
    return value.reshape(value.shape[0], -1, W)


def one_hot(rows, cols, target):
    row = lax.broadcasted_iota(jnp.int32, (rows, cols), 0)
    col = lax.broadcasted_iota(jnp.int32, (rows, cols), 1)
    return jnp.where(row == target(col), 1.0, 0.0).astype(BF16)


def to_inside():
    return one_hot(2 * R, 2 * R, lambda n: (n & 7) * C + (n >> 3))


def to_outside():
    return one_hot(2 * R, 2 * R, lambda n: (n & (C - 1)) * 8 + (n >> 5))


def reorder(matrix, pieces):
    both = jnp.dot(matrix, jnp.concatenate(pieces, axis=1), preferred_element_type=F32).astype(BF16)
    return [both[:, k * W : (k + 1) * W] for k in range(len(pieces))]


def prepare_kernel(fwd_hbm, acts_hbm, grads_hbm, nat, fwd, acts, grads, sems):
    pairs = ((fwd_hbm, fwd), (acts_hbm, acts), (grads_hbm, grads))
    copies = [pltpu.make_async_copy(src, dst, sems.at[k]) for k, (src, dst) in enumerate(pairs)]
    for copy in copies:
        copy.start()
    order = to_inside()
    for copy in copies:
        copy.wait()
    streams = reorder(order, [acts[0], grads[1], acts[1], grads[0], fwd[1], fwd[0]])
    for k, v in enumerate(streams):
        nat[2 * k] = v[:R]
        nat[2 * k + 1] = v[R:]


def prepare_ends_kernel(flags, batch, loss, nat, first_own, last_own, ends, near, nat_x2):
    zh = flags[0]
    move([
        (at(nat, 0, 4), at(near, 0, 4)),
        (at(nat, 8, 4), at(near, 4, 4)),
        (at(nat, 4 + zh, 1), at(near, 8, 1)),
        (at(nat, 6 + zh, 1), at(near, 9, 1)),
        (at(nat, 8, 2), nat_x2),
    ])
    x1, x2, d1, d2 = reorder(to_inside(), [batch[0], batch[1], loss[0], loss[1]])
    for ref, pair in ((first_own, (x1, x2)), (last_own, (d1, d2))):
        for k in range(2):
            ref[k, 0] = pair[k][:R]
            ref[k, 1] = pair[k][R:]
    first = flags[5] == 1

    @pl.when(first)
    def _():
        ends[...] = first_own[...]

    @pl.when(jnp.logical_not(first))
    def _():
        ends[...] = last_own[...]


def matrices(flat):
    k = flat.reshape(2, C, C, 3, 3, 3)
    turned = jnp.flip(k, (3, 4, 5)).transpose(0, 2, 1, 3, 4, 5)
    both = jnp.concatenate([k, turned])
    rows = both.transpose(0, 5, 1, 3, 4, 2)
    rows = jnp.pad(rows, ((0, 0), (0, 0), (0, 0), (0, 0), (0, 1), (0, 0))).reshape(4, 3, C, 3 * R)
    (out,) = call(bands_kernel, [((4, 3 * R, 3 * R), BF16)], [], (rows,), 1_000_000, [VMEM], [VMEM])
    return out


def local(fwd_in, back_out, back_grad, batch_next, loss_grad, weights):
    seg = lax.axis_index("segment")
    slab = lax.axis_index("slab")
    count = lax.axis_size("segment")
    slabs = lax.axis_size("slab")
    ny = slabs // 2
    y, zh = (slab // 2, slab % 2)
    scale = float(fwd_in.shape[3] * slabs * fwd_in.shape[4] * fwd_in.shape[5]) ** (-0.5)

    def route(value, to):
        pairs = []
        for s in range(count):
            for yy in range(ny):
                for zz in range(2):
                    target = to(s, yy, zz)
                    if target is None:
                        continue
                    ts, ty, tz = target
                    if 0 <= ts < count and 0 <= ty < ny:
                        pairs.append((s * slabs + 2 * yy + zz, ts * slabs + 2 * ty + tz))
        return lax.ppermute(value, ("segment", "slab"), pairs)

    def fwd_side(s, zz):
        return 1 - zz if s % SNAKE == SNAKE - 1 and s < count - 1 else zz

    def back_side(s, zz):
        return 1 - zz if s % SNAKE == 0 and s > 0 else zz

    fz = jnp.where((seg % SNAKE == SNAKE - 1) & (seg < count - 1), 1 - zh, zh)
    is_first, is_last = (seg == 0, seg == count - 1)

    def swap(value):
        return route(value, lambda s, yy, zz: (s, yy, 1 - zz))

    def as_flags(*values):
        return jnp.stack([jnp.asarray(v).astype(jnp.int32) for v in values])

    from_first, from_last = (14 % count, (count - 15) % count)
    flags1 = as_flags(zh, y > 0, y < ny - 1, fz, 0, seg == from_first, is_last)
    flags2 = as_flags(zh, (y > 0) | (zh == 1), (y < ny - 1) | (zh == 0), is_first, is_last)
    (nat,) = call(
        prepare_kernel,
        [shaped(12)],
        [pltpu.VMEM((2, 2 * R, W), BF16)] * 3 + [pltpu.SemaphoreType.DMA((3,))],
        (flat_rows(fwd_in[0]), flat_rows(back_out[0]), flat_rows(back_grad[0])),
        100_000_000,
        [HBM] * 3,
        [VMEM],
        58,
    )
    swp = swap(nat)
    first_own, last_own, ends, near, nat_x2 = call(
        prepare_ends_kernel,
        [shaped(2, 2)] * 3 + [shaped(10), shaped(2)],
        [],
        (flags1, flat_rows(batch_next), flat_rows(loss_grad[0]), nat),
        100_000_000,
        [SMEM] + [VMEM] * 3,
        [VMEM] * 5,
    )

    near = route(near, lambda s, yy, zz: (s, yy - 1 + 2 * zz, zz))
    e1 = route(nat_x2, lambda s, yy, zz: (s if s == count - 1 else -1, yy + 1 - 2 * zz, zz))
    e2 = route(nat_x2, lambda s, yy, zz: (s if s == count - 1 else -1, yy + 1 - 2 * zz, 1 - zz))

    def end_of(s):
        return 0 if s == from_first else count - 1 if s == from_last else -1

    sp1 = route(ends, lambda s, yy, zz: (end_of(s), yy, 1 - zz))
    sp2 = route(ends, lambda s, yy, zz: (end_of(s), yy + (1 if zz == 1 else -1), 1 - zz))
    sp3 = route(last_own, lambda s, yy, zz: (count - 1 if s == count - 2 else -1, yy - 1 + 2 * zz, zz))
    mats = matrices(weights[0])


    swp, near, sp1, sp2, sp3, e1, e2, mats = lax.optimization_barrier((swp, near, sp1, sp2, sp3, e1, e2, mats))

    far = route(swp, lambda s, yy, zz: (s, yy + 1 - 2 * zz, zz))
    bm, bl, bh, dw = call(
        tick1_back,
        [shaped(20), shaped(4), shaped(4), ((2, 9 * C, 3 * C), F32)],
        [planes(8), planes(6), planes(8), planes(6), planes(6), planes(4), planes(6), planes(4), planes(8), planes(6)],
        (flags1, mats, nat, swp, near, far),
        2_000_000_000,
        [SMEM] + [VMEM] * 5,
        [VMEM] * 4,
    )

    def fwd_diag(s, yy, zz):
        r = fwd_side(s, zz)
        return (s + 1, yy + 1 - 2 * r, r)

    bm2 = route(bm, lambda s, yy, zz: (s - 1, yy, back_side(s, zz)))
    bl2 = route(bl, lambda s, yy, zz: (s - 1, yy + 1, back_side(s, zz)))
    bh2 = route(bh, lambda s, yy, zz: (s - 1, yy - 1, back_side(s, zz)))

    fm, fd, own = call(
        tick1_forward,
        [shaped(8), shaped(2), shaped(18)],
        [planes(10), planes(8), planes(8), planes(6), planes(10), planes(8)],
        (flags1, mats, nat, swp, near, far, last_own, e1, e2),
        1_000_000_000,
        [SMEM] + [VMEM] * 8,
        [VMEM] * 3,
    )
    fd2 = route(fd, fwd_diag)
    fm2 = route(fm, lambda s, yy, zz: (s + 1, yy, fwd_side(s, zz)))

    bm2, bl2, bh2, fd2 = lax.optimization_barrier((bm2, bl2, bh2, fd2))
    out_b, parts = call(
        functools.partial(tick2_back, scale),
        [((4, 2 * R, W), BF16), ((ny, slab_rows(slabs), W), BF16)],
        [planes(8), planes(6), planes(8), planes(6), planes(6), planes(4), planes(6), planes(4), planes(8), planes(6)],
        (flags1, mats, bm2, bl2, bh2, sp1, sp2, sp3, own, dw),
        1_500_000_000,
        [SMEM] + [VMEM] * 9,
        [VMEM, VMEM],
    )
    back = route(out_b, lambda s, yy, zz: (s - 1, yy, zz))
    columns = [[2 * k + j for k in range(ny)] for j in range(2)]
    parts = lax.all_to_all(parts, "slab", 0, 0, axis_index_groups=columns, tiled=True)

    fm2, out_b = lax.optimization_barrier((fm2, out_b))
    (out_f,) = call(
        tick2_forward,
        [((2, 2 * R, W), BF16)],
        [planes(6), planes(4), planes(4), planes(2), planes(6), planes(4)],
        (flags2, mats, fm2, fd2, sp1, sp2, first_own),
        700_000_000,
        [SMEM] + [VMEM] * 6,
        [VMEM],
    )

    total = jnp.sum(wide(parts), axis=0)[: 2 * 9 * (C // slabs), : 3 * C]
    total = total.reshape(2, 9, C // slabs, 3, C).transpose(0, 4, 2, 1, 3).reshape(1, 2, C, -1)

    acts = jnp.where(is_last, out_f, back[:2])
    grads = jnp.where(is_last, flat_rows(loss_grad[1]), back[2:])
    return (*(v.reshape(fwd_in.shape) for v in (out_f, acts, grads)), total)


def solution(mesh):
    placed = (
        P("segment", None, None, "slab", None, None),
        P("segment", None, None, "slab", None, None),
        P("segment", None, None, "slab", None, None),
        P(None, None, "slab", None, None),
        P(None, None, None, "slab", None, None),
        P("segment", None, None, None),
    )
    return jax.shard_map(
        local,
        mesh=mesh,
        in_specs=placed,
        out_specs=(
            P("segment", None, None, "slab", None, None),
            P("segment", None, None, "slab", None, None),
            P("segment", None, None, "slab", None, None),
            P("segment", None, None, "slab"),
        ),
        check_vma=False,
    )
```

```python
import functools

import jax
import jax.numpy as jnp
from jax import lax
from jax.experimental import pallas as pl
from jax.experimental.pallas import tpu as pltpu
from jax.sharding import PartitionSpec as P

F32 = jnp.float32
BF16 = jnp.bfloat16
C = 32
H = 4
R = C * H
W = 128
SNAKE = 16


def wide(v):
    return v.astype(F32)


def silu(v):
    v = wide(v)
    return (v / (1.0 + jnp.exp(-v))).astype(BF16)


def slope(v):
    v = wide(v)
    sig = 1.0 / (1.0 + jnp.exp(-v))
    return sig * (1.0 + v * (1.0 - sig))


def conv_planes(w_ref, field, start, count, use):
    lane = lax.broadcasted_iota(jnp.int32, (R, W), 1)
    for d in range(0, count, 2):
        n = min(2, count - d)
        x = jnp.concatenate(
            [jnp.concatenate([field[start + d + k + a] for a in range(3)], axis=0) for k in range(n)], axis=1
        )
        y = jnp.dot(w_ref[...], x, preferred_element_type=F32)
        for k in range(n):
            cols = slice(k * W, (k + 1) * W)
            left = jnp.where(lane >= 1, pltpu.roll(y[:R, cols], 1, 1), 0.0)
            right = jnp.where(lane < W - 1, pltpu.roll(y[2 * R :, cols], W - 1, 1), 0.0)
            use(start + d + k, y[R : 2 * R, cols] + left + right)


def mask(d, v, inner, keep, edge=1):
    if d < edge:
        v = v * keep[0]
    if d >= inner - edge:
        v = v * keep[1]
    return v


def forward(n, keep, w_ref, fb, fa, out_a, out_b, act_b, act_a):
    inner = n - 2
    for p in range(n):
        act_b[p] = silu(fb[p])

    def one(d, v):
        out = mask(d, wide(fa[d]) + v, inner, keep, max(1, n - 8)).astype(BF16)
        out_a[d] = out
        act_a[d] = silu(out)

    conv_planes(w_ref.at[0], act_b, 0, inner, one)

    def two(d, v):
        out_b[d] = (wide(fb[d + 2]) + v).astype(BF16)

    conv_planes(w_ref.at[1], act_a, 0, inner - 2, two)


def backward(keep, w_ref, bb, ba, db, da, rec_a, rec_b, grad_a, grad_b, act_b, act_a, first, count):
    n, inner = (8, 6)
    for p in range(n):
        act_b[p] = silu(bb[p])

    def one(d, v):
        out = mask(d, wide(ba[d]) - v, inner, keep).astype(BF16)
        rec_a[d] = out
        act_a[d] = silu(out)

    conv_planes(w_ref.at[1], act_b, 0, inner, one)

    def two(d, v):
        grad_a[d] = mask(d, wide(da[d]) + slope(bb[d + 1]) * v, inner, keep).astype(BF16)

    conv_planes(w_ref.at[3], db, 0, inner, two)

    def three(d, v):
        rec_b[d] = (wide(bb[d + 2]) - v).astype(BF16)

    conv_planes(w_ref.at[0], act_a, first, count, three)

    def four(d, v):
        grad_b[d] = (wide(db[d + 2]) + slope(rec_a[d + 1]) * v).astype(BF16)

    conv_planes(w_ref.at[2], grad_a, first, count, four)


def move(pairs):
    for src, dst in pairs:
        for k in range(dst.shape[0]):
            dst[k] = src[k]


def at(ref, first, count):
    return ref.at[pl.ds(first, count)]


def window1(zh, b, a, nat_b, nat_a, swp_b, swp_a, near_b, near_a, far_b, far_a):
    return [
        (nat_b, at(b, 2 + 2 * zh, 2)),
        (swp_b, at(b, 4 - 2 * zh, 2)),
        (near_b, at(b, 6 - 6 * zh, 2)),
        (far_b, at(b, 6 * zh, 2)),
        (nat_a, at(a, 1 + 2 * zh, 2)),
        (swp_a, at(a, 3 - 2 * zh, 2)),
        (near_a, at(a, 5 - 5 * zh, 1)),
        (far_a, at(a, 5 * zh, 1)),
    ]


def special(zh, b, a, own, sp1, sp2):
    return [
        (own[1], at(b, 2, 2)),
        (sp1.at[1], at(b, 4 - 4 * zh, 2)),
        (sp2.at[1], at(b, 4 * zh, 2)),
        (own[0], at(a, 1, 2)),
        (at(sp1.at[0], zh, 1), at(a, 3 - 3 * zh, 1)),
        (at(sp2.at[0], 1 - zh, 1), at(a, 3 * zh, 1)),
    ]


def keeps(flags):
    return (flags[1].astype(F32), flags[2].astype(F32))


def weight_sums(db, grad_a, act_b, act_a):
    return (
        wgrad_pair(at(grad_a, 1, 4), act_a),
        wgrad_pair(at(db, 2, 4), at(act_b, 1, 6)),
    )


def tick1_window(zh, b, a, b_at, a_at, near_b, near_a, nat, swp, near, far):
    move(
        window1(
            zh, b, a, at(nat, b_at, 2), at(nat, a_at, 2), at(swp, b_at, 2), at(swp, a_at, 2),
            at(near, near_b, 2), at(near, near_a, 1), at(far, b_at, 2), at(far, a_at + 1 - zh, 1),
        )
    )


def tick1_back(flags, w_ref, nat, swp, near, far, bm, bl, bh, dw, *scratch):
    bb, ba, db, da, rec_a, rec_b, grad_a, grad_b, act_b, act_a = scratch
    for k, (b, a) in enumerate(((bb, ba), (db, da))):
        tick1_window(flags[0], b, a, 2 * k, 4 + 2 * k, 2 * k, 8 + k, nat, swp, near, far)
    backward(keeps(flags), w_ref, bb, ba, db, da, rec_a, rec_b, grad_a, grad_b, act_b, act_a, 0, 4)
    move([
        (rec_b, at(bm, 0, 4)),
        (grad_b, at(bm, 4, 4)),
        (rec_a, at(bm, 8, 6)),
        (grad_a, at(bm, 14, 6)),
        (at(rec_b, 2, 2), at(bl, 0, 2)),
        (at(grad_b, 2, 2), at(bl, 2, 2)),
        (at(rec_b, 0, 2), at(bh, 0, 2)),
        (at(grad_b, 0, 2), at(bh, 2, 2)),
    ])
    dw[0], dw[1] = weight_sums(db, grad_a, act_b, act_a)


def tick1_forward(flags, w_ref, nat, swp, near, far, last_own, e1, e2, fm, fd, own, *scratch):
    fb, fa, out_a, out_b, act_b, act_a = scratch
    zh, fz = (flags[0], flags[3])

    @pl.when(flags[6] == 0)
    def _():
        tick1_window(zh, fb, fa, 8, 10, 4, 6 + zh, nat, swp, near, far)
        forward(8, keeps(flags), w_ref, fb, fa, out_a, out_b, act_b, act_a)
        move([
            (at(out_b, 0, 4), at(fm, 0, 4)),
            (at(out_a, 2 * fz, 4), at(fm, 4, 4)),
            (at(out_b, 2 - 2 * fz, 2), fd),
        ])

    @pl.when(flags[6] == 1)
    def _():
        for win, k in ((at(fb, 1, 8), 8), (fa, 10)):
            move([
                (at(nat, k, 2), at(win, 2 + 2 * zh, 2)),
                (at(swp, k, 2), at(win, 4 - 2 * zh, 2)),
                (at(near, k - 4, 2), at(win, 6 - 6 * zh, 2)),
                (at(far, k, 2), at(win, 6 * zh, 2)),
            ])
        move([(at(e1, 1 - zh, 1), at(fb, 9 * zh, 1)), (at(e2, zh, 1), at(fb, 9 - 9 * zh, 1))])
        forward(10, keeps(flags), w_ref, fb, fa, out_a, out_b, act_b, act_a)
        move([
            (out_a, at(own, 0, 8)),
            (out_b, at(own, 8, 6)),
            (last_own.at[0], at(own, 14, 2)),
            (last_own.at[1], at(own, 16, 2)),
        ])


def tick2_back(
    scale, flags, w_ref, bm, bl, bh, sp1, sp2, sp3, own, dw, out, parts, *scratch
):
    bb, ba, db, da, rec_a, rec_b, grad_a, grad_b, act_b, act_a = scratch
    zh = flags[0]

    @pl.when(flags[6] == 1)
    def _():
        move(window1(
            zh, db, da, at(own, 16, 2), at(own, 14, 2), sp1.at[1], sp1.at[0],
            sp3.at[1], at(sp3.at[0], zh, 1), sp2.at[1], at(sp2.at[0], 1 - zh, 1),
        ))
        move([
            (at(own, 0, 8), bb),
            (at(own, 8, 6), ba),
        ])

    @pl.when(flags[6] == 0)
    def _():
        move([
            (at(bl, 0, 2), at(bb, 0, 2)),
            (at(bm, 0, 4), at(bb, 2, 4)),
            (at(bh, 0, 2), at(bb, 6, 2)),
            (at(bl, 2, 2), at(db, 0, 2)),
            (at(bm, 4, 4), at(db, 2, 4)),
            (at(bh, 2, 2), at(db, 6, 2)),
            (at(bm, 8, 6), ba),
            (at(bm, 14, 6), da),
        ])

    order, back_order = (slab_order(2 * parts.shape[0], zh), to_outside())
    backward(keeps(flags), w_ref, bb, ba, db, da, rec_a, rec_b, grad_a, grad_b, act_b, act_a, 2 * zh, 2)
    own_a, own_b = (pl.ds(1 + 2 * zh, 2), pl.ds(2 * zh, 2))
    pieces = [rec_b[own_b], rec_a[own_a], grad_a[own_a], grad_b[own_b]]
    for k, v in enumerate(reorder(back_order, [p.reshape(2 * R, W) for p in pieces])):
        out[k] = v
    sums = [dw[k] + v for k, v in enumerate(weight_sums(db, grad_a, act_b, act_a))]
    sums = jnp.concatenate([(v * scale).astype(BF16) for v in sums], axis=0)
    ordered = jnp.dot(order, sums, preferred_element_type=F32).astype(BF16)
    parts[:, :, : 3 * C] = ordered.reshape(*parts.shape[:2], 3 * C)
    parts[:, :, 3 * C :] = jnp.zeros((*parts.shape[:2], W - 3 * C), BF16)


def tick2_forward(flags, w_ref, fm, fd, sp1, sp2, first_own, out, *scratch):
    fb, fa, out_a, out_b, act_b, act_a = scratch
    zh, first = (flags[0], flags[3])

    @pl.when(first == 1)
    def _():
        move(special(zh, fb, fa, (first_own.at[0], first_own.at[1]), sp1, sp2))

    @pl.when(first == 0)
    def _():
        move([(at(fm, 0, 4), at(fb, 2 - 2 * zh, 4)), (fd, at(fb, 4 * zh, 2)), (at(fm, 4, 4), fa)])

    forward(6, keeps(flags), w_ref, fb, fa, out_a, out_b, act_b, act_a)
    for k, v in enumerate(reorder(to_outside(), [p.reshape(2 * R, W) for p in (out_a[1:3], out_b[...])])):
        out[k] = v


def wgrad_pair(g_ref, u_ref):
    lane = lax.broadcasted_iota(jnp.int32, (C, W), 1)
    zero = jnp.zeros((C, W), BF16)
    left, right = ([], [])
    for d in range(g_ref.shape[0]):
        for h in range(H):
            g = wide(g_ref[d, h * C : (h + 1) * C])
            down = jnp.where(lane < W - 1, pltpu.roll(g, W - 1, 1), 0.0)
            up = jnp.where(lane >= 1, pltpu.roll(g, 1, 1), 0.0)
            left.append(jnp.concatenate([down, g, up], axis=0).astype(BF16))
            rows = []
            for a in range(3):
                for b in range(3):
                    at = h + b - 1
                    rows.append(u_ref[d + a, at * C : (at + 1) * C] if 0 <= at < H else zero)
            right.append(jnp.concatenate(rows, axis=0))
    return lax.dot_general(
        jnp.concatenate(right, axis=1),
        jnp.concatenate(left, axis=1),
        (((1,), (1,)), ((), ())),
        preferred_element_type=F32,
    )


def bands_kernel(rows, out):
    lane = lax.broadcasted_iota(jnp.int32, (C, R), 1)
    for kind in range(4):
        for c in range(3):
            for a in range(3):
                tile = wide(rows[kind, c, :, a * R : (a + 1) * R])
                for h in range(H):
                    moved = tile if h == 1 else pltpu.roll(tile, ((h - 1) * C) % R, 1)
                    if h == 0:
                        moved = jnp.where(lane < 2 * C, moved, 0.0)
                    if h == 3:
                        moved = jnp.where(lane >= 2 * C, moved, 0.0)
                    at_row = (c * H + h) * C
                    out[kind, at_row : at_row + C, a * R : (a + 1) * R] = moved.astype(BF16)


VMEM = pl.BlockSpec(memory_space=pltpu.VMEM)
SMEM = pl.BlockSpec(memory_space=pltpu.SMEM)
HBM = pl.BlockSpec(memory_space=pltpu.HBM)


def call(kernel, outs, scratch, args, flops, specs, out_specs, mib=16):
    return pl.pallas_call(
        kernel,
        out_shape=tuple(jax.ShapeDtypeStruct(s, t) for s, t in outs),
        in_specs=specs,
        out_specs=tuple(out_specs),
        scratch_shapes=scratch,
        compiler_params=pltpu.CompilerParams(vmem_limit_bytes=mib * 2**20),
        cost_estimate=pl.CostEstimate(flops=flops, bytes_accessed=4_000_000, transcendentals=400_000),
    )(*args)


def slab_rows(slabs):
    return -(-2 * 9 * C // (16 * slabs)) * 16


def slab_order(slabs, zh):
    per = C // slabs
    low, rows = (per.bit_length() - 1, slab_rows(slabs))

    def target(n):
        slab = (n & (C - 1)) >> low
        row = (slab >> 1) * rows + (n >> 5) * per + (n & (per - 1))
        return jnp.where((slab & 1) == zh, row, -1)

    return one_hot(slabs // 2 * rows, 2 * 9 * C, target)


def planes(*lead):
    return pltpu.VMEM((*lead, R, W), BF16)


def shaped(*lead):
    return ((*lead, R, W), BF16)


def flat_rows(value):
    return value.reshape(value.shape[0], -1, W)


def one_hot(rows, cols, target):
    row = lax.broadcasted_iota(jnp.int32, (rows, cols), 0)
    col = lax.broadcasted_iota(jnp.int32, (rows, cols), 1)
    return jnp.where(row == target(col), 1.0, 0.0).astype(BF16)


def to_inside():
    return one_hot(2 * R, 2 * R, lambda n: (n & 7) * C + (n >> 3))


def to_outside():
    return one_hot(2 * R, 2 * R, lambda n: (n & (C - 1)) * 8 + (n >> 5))


def reorder(matrix, pieces):
    both = jnp.dot(matrix, jnp.concatenate(pieces, axis=1), preferred_element_type=F32).astype(BF16)
    return [both[:, k * W : (k + 1) * W] for k in range(len(pieces))]


def prepare_kernel(fwd_hbm, acts_hbm, grads_hbm, nat, fwd, acts, grads, sems):
    pairs = ((fwd_hbm, fwd), (acts_hbm, acts), (grads_hbm, grads))
    copies = [pltpu.make_async_copy(src, dst, sems.at[k]) for k, (src, dst) in enumerate(pairs)]
    for copy in copies:
        copy.start()
    order = to_inside()
    for copy in copies:
        copy.wait()
    streams = reorder(order, [acts[0], grads[1], acts[1], grads[0], fwd[1], fwd[0]])
    for k, v in enumerate(streams):
        nat[2 * k] = v[:R]
        nat[2 * k + 1] = v[R:]


def prepare_ends_kernel(flags, batch, loss, nat, first_own, last_own, ends, near, nat_x2):
    zh = flags[0]
    move([
        (at(nat, 0, 4), at(near, 0, 4)),
        (at(nat, 8, 4), at(near, 4, 4)),
        (at(nat, 4 + zh, 1), at(near, 8, 1)),
        (at(nat, 6 + zh, 1), at(near, 9, 1)),
        (at(nat, 8, 2), nat_x2),
    ])
    x1, x2, d1, d2 = reorder(to_inside(), [batch[0], batch[1], loss[0], loss[1]])
    for ref, pair in ((first_own, (x1, x2)), (last_own, (d1, d2))):
        for k in range(2):
            ref[k, 0] = pair[k][:R]
            ref[k, 1] = pair[k][R:]
    first = flags[5] == 1

    @pl.when(first)
    def _():
        ends[...] = first_own[...]

    @pl.when(jnp.logical_not(first))
    def _():
        ends[...] = last_own[...]


def matrices(flat):
    k = flat.reshape(2, C, C, 3, 3, 3)
    turned = jnp.flip(k, (3, 4, 5)).transpose(0, 2, 1, 3, 4, 5)
    both = jnp.concatenate([k, turned])
    rows = both.transpose(0, 5, 1, 3, 4, 2)
    rows = jnp.pad(rows, ((0, 0), (0, 0), (0, 0), (0, 0), (0, 1), (0, 0))).reshape(4, 3, C, 3 * R)
    (out,) = call(bands_kernel, [((4, 3 * R, 3 * R), BF16)], [], (rows,), 1_000_000, [VMEM], [VMEM])
    return out


def local(fwd_in, back_out, back_grad, batch_next, loss_grad, weights):
    seg = lax.axis_index("segment")
    slab = lax.axis_index("slab")
    count = lax.axis_size("segment")
    slabs = lax.axis_size("slab")
    ny = slabs // 2
    y, zh = (slab // 2, slab % 2)
    scale = float(fwd_in.shape[3] * slabs * fwd_in.shape[4] * fwd_in.shape[5]) ** (-0.5)

    def route(value, to):
        pairs = []
        for s in range(count):
            for yy in range(ny):
                for zz in range(2):
                    target = to(s, yy, zz)
                    if target is None:
                        continue
                    ts, ty, tz = target
                    if 0 <= ts < count and 0 <= ty < ny:
                        pairs.append((s * slabs + 2 * yy + zz, ts * slabs + 2 * ty + tz))
        return lax.ppermute(value, ("segment", "slab"), pairs)

    def fwd_side(s, zz):
        return 1 - zz if s % SNAKE == SNAKE - 1 and s < count - 1 else zz

    def back_side(s, zz):
        return 1 - zz if s % SNAKE == 0 and s > 0 else zz

    fz = jnp.where((seg % SNAKE == SNAKE - 1) & (seg < count - 1), 1 - zh, zh)
    is_first, is_last = (seg == 0, seg == count - 1)

    def swap(value):
        return route(value, lambda s, yy, zz: (s, yy, 1 - zz))

    def as_flags(*values):
        return jnp.stack([jnp.asarray(v).astype(jnp.int32) for v in values])

    from_first, from_last = (14 % count, (count - 15) % count)
    flags1 = as_flags(zh, y > 0, y < ny - 1, fz, 0, seg == from_first, is_last)
    flags2 = as_flags(zh, (y > 0) | (zh == 1), (y < ny - 1) | (zh == 0), is_first, is_last)
    (nat,) = call(
        prepare_kernel,
        [shaped(12)],
        [pltpu.VMEM((2, 2 * R, W), BF16)] * 3 + [pltpu.SemaphoreType.DMA((3,))],
        (flat_rows(fwd_in[0]), flat_rows(back_out[0]), flat_rows(back_grad[0])),
        100_000_000,
        [HBM] * 3,
        [VMEM],
        58,
    )
    swp = swap(nat)
    first_own, last_own, ends, near, nat_x2 = call(
        prepare_ends_kernel,
        [shaped(2, 2)] * 3 + [shaped(10), shaped(2)],
        [],
        (flags1, flat_rows(batch_next), flat_rows(loss_grad[0]), nat),
        100_000_000,
        [SMEM] + [VMEM] * 3,
        [VMEM] * 5,
    )

    near = route(near, lambda s, yy, zz: (s, yy - 1 + 2 * zz, zz))
    e1 = route(nat_x2, lambda s, yy, zz: (s if s == count - 1 else -1, yy + 1 - 2 * zz, zz))
    e2 = route(nat_x2, lambda s, yy, zz: (s if s == count - 1 else -1, yy + 1 - 2 * zz, 1 - zz))

    def end_of(s):
        return 0 if s == from_first else count - 1 if s == from_last else -1

    sp1 = route(ends, lambda s, yy, zz: (end_of(s), yy, 1 - zz))
    sp2 = route(ends, lambda s, yy, zz: (end_of(s), yy + (1 if zz == 1 else -1), 1 - zz))
    sp3 = route(last_own, lambda s, yy, zz: (count - 1 if s == count - 2 else -1, yy - 1 + 2 * zz, zz))
    mats = matrices(weights[0])


    swp, near, sp1, sp2, sp3, e1, e2, mats = lax.optimization_barrier((swp, near, sp1, sp2, sp3, e1, e2, mats))

    far = route(swp, lambda s, yy, zz: (s, yy + 1 - 2 * zz, zz))
    bm, bl, bh, dw = call(
        tick1_back,
        [shaped(20), shaped(4), shaped(4), ((2, 9 * C, 3 * C), F32)],
        [planes(8), planes(6), planes(8), planes(6), planes(6), planes(4), planes(6), planes(4), planes(8), planes(6)],
        (flags1, mats, nat, swp, near, far),
        2_000_000_000,
        [SMEM] + [VMEM] * 5,
        [VMEM] * 4,
    )

    def fwd_diag(s, yy, zz):
        r = fwd_side(s, zz)
        return (s + 1, yy + 1 - 2 * r, r)

    bm2 = route(bm, lambda s, yy, zz: (s - 1, yy, back_side(s, zz)))
    bl2 = route(bl, lambda s, yy, zz: (s - 1, yy + 1, back_side(s, zz)))
    bh2 = route(bh, lambda s, yy, zz: (s - 1, yy - 1, back_side(s, zz)))

    fm, fd, own = call(
        tick1_forward,
        [shaped(8), shaped(2), shaped(18)],
        [planes(10), planes(8), planes(8), planes(6), planes(10), planes(8)],
        (flags1, mats, nat, swp, near, far, last_own, e1, e2),
        1_000_000_000,
        [SMEM] + [VMEM] * 8,
        [VMEM] * 3,
    )
    fd2 = route(fd, fwd_diag)
    fm2 = route(fm, lambda s, yy, zz: (s + 1, yy, fwd_side(s, zz)))

    bm2, bl2, bh2 = lax.optimization_barrier((bm2, bl2, bh2))
    out_b, parts = call(
        functools.partial(tick2_back, scale),
        [((4, 2 * R, W), BF16), ((ny, slab_rows(slabs), W), BF16)],
        [planes(8), planes(6), planes(8), planes(6), planes(6), planes(4), planes(6), planes(4), planes(8), planes(6)],
        (flags1, mats, bm2, bl2, bh2, sp1, sp2, sp3, own, dw),
        1_500_000_000,
        [SMEM] + [VMEM] * 9,
        [VMEM, VMEM],
    )
    back = route(out_b, lambda s, yy, zz: (s - 1, yy, zz))
    columns = [[2 * k + j for k in range(ny)] for j in range(2)]
    parts = lax.all_to_all(parts, "slab", 0, 0, axis_index_groups=columns, tiled=True)

    fm2, out_b = lax.optimization_barrier((fm2, out_b))
    (out_f,) = call(
        tick2_forward,
        [((2, 2 * R, W), BF16)],
        [planes(6), planes(4), planes(4), planes(2), planes(6), planes(4)],
        (flags2, mats, fm2, fd2, sp1, sp2, first_own),
        700_000_000,
        [SMEM] + [VMEM] * 6,
        [VMEM],
    )

    total = jnp.sum(wide(parts), axis=0)[: 2 * 9 * (C // slabs), : 3 * C]
    total = total.reshape(2, 9, C // slabs, 3, C).transpose(0, 4, 2, 1, 3).reshape(1, 2, C, -1)

    acts = jnp.where(is_last, out_f, back[:2])
    grads = jnp.where(is_last, flat_rows(loss_grad[1]), back[2:])
    return (*(v.reshape(fwd_in.shape) for v in (out_f, acts, grads)), total)


def solution(mesh):
    placed = (
        P("segment", None, None, "slab", None, None),
        P("segment", None, None, "slab", None, None),
        P("segment", None, None, "slab", None, None),
        P(None, None, "slab", None, None),
        P(None, None, None, "slab", None, None),
        P("segment", None, None, None),
    )
    return jax.shard_map(
        local,
        mesh=mesh,
        in_specs=placed,
        out_specs=(
            P("segment", None, None, "slab", None, None),
            P("segment", None, None, "slab", None, None),
            P("segment", None, None, "slab", None, None),
            P("segment", None, None, "slab"),
        ),
        check_vma=False,
    )
```
